128 devices in a mesh: expert: 64 (over x, z, y_lo, core), dp: 2 (over y_hi).
Axes of the slice: x: 4, y: 4 (y_hi: 2, y_lo: 2; y = y_hi * 2 + y_lo), z: 4, core: 2. Of those that a mesh axis runs over, the one named last changes fastest.
Arguments:
- tokens: bfloat16 [16384, 6144], P(('expert', 'dp')), may hold values from -6 to 6
- cotangent: bfloat16 [16384, 6144], P(('expert', 'dp')), may hold values from -0.59765625 to 0.59765625
- gate_probs: float32 [16384, 2], P(('expert', 'dp')), may hold values from 0.2 to 1
- routes: int32 [16384, 2], P(('expert', 'dp')), may hold values from 0 to 63, all different within a row; in each aligned block of 128 rows (0 to 127, 128 to 255, ...) at most 6 rows name the same one
- placement: int32 [64], replicated, may hold values from 0 to 63, each once
- weights: bfloat16 [64, 6144, 384], P('expert'), may hold values from -1.1 to 1.1, as said below
- first_moment: bfloat16 [64, 6144, 384], P('expert', 'dp'), may hold values from -1.796875 to 1.796875
- second_moment: bfloat16 [64, 6144, 384], P('expert', 'dp'), may hold values from 0.0099487305 to 1
Outputs:
- mixed: bfloat16 [16384, 6144], P(('expert', 'dp'))
- token_grad: bfloat16 [16384, 6144], P(('expert', 'dp'))
- first_new: bfloat16 [64, 6144, 384], P('expert', 'dp')
- second_new: bfloat16 [64, 6144, 384], P('expert', 'dp')
- adam_step: bfloat16 [64, 6144, 384], P('expert', 'dp')
The draws below stay inside these ranges and needn't reach their ends.
Inputs may be any that keep to these rules, and one draw needn't show every extreme that they name: `routes`: each row names 2 different experts; among the rows of one device no expert is named more than 6 times, and that count is reached. `placement`: a permutation of the experts. `weights`: gate and up columns spread about 1/sqrt(6144), down columns about 1/sqrt(128).
All inputs are finite; a program needn't handle non-finite values.
Results may differ from the reference program's by a relative error of at most 0.018.
Values may be sent and summed in bfloat16 or wider, within the bound.
No kernel may reach another device: no remote copies, remote signals or barrier semaphores. Data moves between devices by JAX's collectives and lax.ppermute only.
A program may use at most 192 MiB of HBM per device.

```python
import math
import jax
import jax.numpy as jnp
import numpy as np
from jax import lax

D = 6144
H = 128
TOP = 2
TOK_DEV = 128
EXPERTS = 64
CAP = 6
TOKENS = 16384
N_EXPERT = 64
N_DP = 2


def draw_weights(key, part):
    key = jax.random.fold_in(key, 11)
    shape = (EXPERTS, D, 3 * H)
    column = jnp.arange(3 * H)
    scale = jnp.where(column < 2 * H, D ** (-0.5), H ** (-0.5)).astype(jnp.float32)
    base = jnp.clip(jax.random.normal(key, shape, jnp.float32), -6.0, 6.0)
    return (base * scale[None, None, :]).astype(jnp.bfloat16)


def shard_levels(own_key, dims, pieces, least, largest):
    loudness, own = 1.0, jax.random.fold_in(own_key, 6)
    for position, parts in pieces:
        steps = jnp.exp(jax.random.uniform(jax.random.fold_in(own, position), (parts,), jnp.float32, least / len(pieces), largest / len(pieces)))
        loudness = loudness * jnp.repeat(steps, dims[position] // parts).reshape([-1 if axis == position else 1 for axis in range(len(dims))])
    return loudness


def routed_block(stream_key, own, number, rows, amount, top, limit, lean):
    order = jax.random.permutation(stream_key, amount)
    crowded, common = portions_of(amount, rows * top, limit, lean, True), portions_of(amount, rows * top, limit, lean, False)
    places = jnp.arange(amount)

    def named(lengths, turn):
        used = int((lengths > 0).sum())
        fixed = max(1, used // 4)
        passed = fixed + (places - fixed + turn * (used - fixed)) % max(1, amount - fixed)
        return jnp.zeros((amount,), jnp.int32).at[order[jnp.where(places < fixed, places, passed)]].set(jnp.asarray(lengths, jnp.int32))

    lengths = jnp.where(number % 4 == 0, named(crowded, number // 4), named(common, number - number // 4 - 1))
    mixed = jax.random.permutation(jax.random.fold_in(own, 3), amount)
    source_of, receiver = mixed[0:amount // 2 * 2:2], mixed[1:amount // 2 * 2:2]
    room = jnp.minimum(lengths[source_of] - 1, limit - lengths[receiver]) // 2
    room = jnp.where((source_of == order[0]) | (receiver == order[0]) | (lengths[receiver] == 0), 0, jnp.maximum(room, 0))
    passed = jax.random.randint(jax.random.fold_in(own, 4), (amount // 2,), 0, 1 << 20) % (room + 1)
    lengths = lengths.at[source_of].add(-passed).at[receiver].add(passed)
    items = jnp.searchsorted(jnp.cumsum(lengths), jnp.arange(rows * top), side="right").astype(jnp.int32)
    grid = items.reshape(top, rows).T
    grid = grid[jax.random.permutation(jax.random.fold_in(own, 1), rows)]
    turn = jax.random.randint(jax.random.fold_in(own, 2), (rows, 1), 0, top)
    return jnp.take_along_axis(grid, (jnp.arange(top)[None, :] + turn) % top, axis=1)


def portions_of(amount, total, bound, skew, full):
    weights = [(1 << 20) // math.isqrt(standing ** skew) + 1 for standing in range(1, amount + 1)]
    largest = bound if full else min(bound, max(-(-total // amount), total * weights[0] // sum(weights)))
    least = 1 if total - largest >= amount - 1 else 0
    holding, spare = [largest] + [least] * (amount - 1), total - largest - least * (amount - 1)
    while spare > 0:
        candidates = [i for i in range(1, amount) if holding[i] < largest] or [i for i in range(1, amount) if holding[i] < bound]
        pool, budget = sum([weights[i] for i in candidates]), spare
        for i in candidates:
            extra = min(bound - holding[i], max(1, budget * weights[i] // pool), spare)
            holding[i] = holding[i] + extra
            spare = spare - extra
    return np.array(holding)


def normal_values(rng, shape, scale, bound, split=(), held_as=jnp.bfloat16):
    values = jax.random.normal(rng, shape, jnp.float32) * scale
    if len(split) > 0:
        values = shard_levels(rng, shape, split, -0.22, 0.18) * values
    return jnp.clip(values, min=-bound, max=bound).astype(held_as)


def setup_inputs(seed: int = 0) -> dict:
    streams_of = jax.random.split(jax.random.key(seed), 9)
    tokens = normal_values(streams_of[0], (TOKENS, D), 1.0, 6.0, ((0, 128),))
    cotangent = normal_values(streams_of[1], (TOKENS, D), 0.1, 0.59765625, ((0, 128),))
    gate_probs = jnp.clip(0.2 + 0.8 * jax.random.uniform(streams_of[2], (TOKENS, TOP), jnp.float32) ** shard_levels(streams_of[2], (TOKENS, TOP), ((0, 128),), -0.2, 0.2), 0.2, 1.0)
    routes_keys = jax.random.split(jax.random.fold_in(streams_of[3], 1), TOKENS // TOK_DEV)
    routes_turns = jax.random.permutation(jax.random.fold_in(streams_of[3], 3), TOKENS // TOK_DEV)
    routes = jax.vmap(lambda own, number: routed_block(jax.random.fold_in(streams_of[3], 2), own, number, TOK_DEV, EXPERTS, TOP, CAP, 2))(routes_keys, routes_turns).reshape((TOKENS, TOP))
    placement = jax.random.permutation(streams_of[4], EXPERTS).astype(jnp.int32)
    weights = draw_weights(jax.random.fold_in(streams_of[8], 71), 0)
    first_moment = normal_values(streams_of[6], (EXPERTS, D, 3 * H), 0.3, 1.796875, ((0, 64), (1, 2)))
    second_moment = jnp.clip(jnp.exp(math.log(1.0) - 4.61031033 * jax.random.uniform(streams_of[7], (EXPERTS, D, 3 * H), jnp.float32) ** shard_levels(streams_of[7], (EXPERTS, D, 3 * H), ((0, 64), (1, 2)), -0.2, 0.2)), 0.0099487305, 1.0).astype(jnp.bfloat16)
    return {"tokens": tokens, "cotangent": cotangent, "gate_probs": gate_probs, "routes": routes, "placement": placement, "weights": weights, "first_moment": first_moment, "second_moment": second_moment}


def expert_pass(weight, row_data, row_cot):
    hidden = weight.shape[1] // 3
    front_both = jnp.dot(row_data, weight[:, :2 * hidden], preferred_element_type=jnp.float32)
    gate_pre = front_both[:, :hidden]
    upward = front_both[:, hidden:]
    sigmoid_gate = jax.nn.sigmoid(gate_pre)
    active = gate_pre * sigmoid_gate
    inner_act = (active * upward).astype(jnp.bfloat16)
    down_cols = weight[:, 2 * hidden:]
    output = lax.dot_general(inner_act, down_cols, (((1,), (1,)), ((), ())), preferred_element_type=jnp.float32).astype(jnp.bfloat16)
    inner_grad = jnp.dot(row_cot, down_cols, preferred_element_type=jnp.float32)
    slope_term = sigmoid_gate * (1.0 + gate_pre * (1.0 - sigmoid_gate))
    pre_grad = jnp.concatenate([inner_grad * upward * slope_term, inner_grad * active], axis=1).astype(jnp.bfloat16)
    grad_front = lax.dot_general(row_data, pre_grad, (((0,), (0,)), ((), ())), preferred_element_type=jnp.float32)
    grad_down = lax.dot_general(row_cot, inner_act, (((0,), (0,)), ((), ())), preferred_element_type=jnp.float32)
    row_grad = lax.dot_general(pre_grad, weight[:, :2 * hidden], (((1,), (1,)), ((), ())), preferred_element_type=jnp.float32).astype(jnp.bfloat16)
    return (output, row_grad, jnp.concatenate([grad_front, grad_down], axis=1))

def adamw(gradient, first_in, second_in, current):
    first_next = 0.9 * first_in.astype(jnp.float32) + 0.1 * gradient
    second_next = 0.95 * second_in.astype(jnp.float32) + 0.05 * gradient * gradient
    step_dir = first_next / (jnp.sqrt(second_next) + 1e-08) + 0.1 * current
    return (first_next.astype(jnp.bfloat16), second_next.astype(jnp.bfloat16), step_dir.astype(jnp.bfloat16))

def reference(tokens, cotangent, gate_probs, routes, placement, weights, first_moment, second_moment):
    blocks = N_EXPERT * N_DP
    per_block = TOK_DEV * TOP
    assigned = TOKENS * TOP
    expert_ids = routes.reshape(blocks, per_block).astype(jnp.int32)
    labels = jnp.arange(EXPERTS, dtype=jnp.int32)
    onehot = (expert_ids[:, :, None] == labels[None, None, :]).astype(jnp.int32)
    earlier = lax.optimization_barrier(jnp.sum((jnp.cumsum(onehot, axis=1) - onehot) * onehot, axis=2)).astype(jnp.int32)
    block_ids = jnp.broadcast_to(jnp.arange(blocks, dtype=jnp.int32)[:, None], (blocks, per_block))
    numbers = jnp.arange(assigned, dtype=jnp.int32).reshape(blocks, per_block)
    table = jnp.full((EXPERTS, blocks, CAP), assigned, jnp.int32).at[expert_ids, block_ids, earlier].set(numbers)
    inverse = jnp.zeros((EXPERTS,), jnp.int32).at[placement].set(labels)
    token_pad = jnp.concatenate([tokens, jnp.zeros((1, D), tokens.dtype)], axis=0)
    cot_pad = jnp.concatenate([cotangent, jnp.zeros((1, D), cotangent.dtype)], axis=0)
    probs_pad = jnp.concatenate([gate_probs.reshape(-1), jnp.zeros((1,), gate_probs.dtype)])

    def one_slot(totals, device):
        out_acc, grad_acc = totals
        expert = inverse[device]
        weight = weights[expert]
        grad_total = jnp.zeros((D, 3 * H), jnp.float32)
        expert_table = table[expert]
        for replica in range(N_DP):
            picked = expert_table[replica::N_DP].reshape(-1)
            row_token = picked // TOP
            row_data = token_pad[row_token]
            row_prob = probs_pad[picked]
            row_cot = (row_prob[:, None] * cot_pad[row_token].astype(jnp.float32)).astype(jnp.bfloat16)
            expert_out, row_grad, gradient = expert_pass(weight, row_data, row_cot)
            rounded = lax.optimization_barrier(gradient.astype(jnp.bfloat16))
            grad_total = grad_total + rounded.astype(jnp.float32)
            out_acc = out_acc.at[row_token].add(row_prob[:, None] * expert_out.astype(jnp.float32))
            grad_acc = grad_acc.at[row_token].add(row_grad.astype(jnp.float32))
        results = adamw(grad_total, first_moment[expert], second_moment[expert], weight.astype(jnp.float32))
        return ((out_acc, grad_acc), results)
    start = (jnp.zeros((TOKENS + 1, D), jnp.float32), jnp.zeros((TOKENS + 1, D), jnp.float32))
    (out_acc, grad_acc), states = lax.scan(one_slot, start, labels)
    mixed = out_acc[:TOKENS].astype(jnp.bfloat16)
    token_grad = grad_acc[:TOKENS].astype(jnp.bfloat16)
    return (mixed, token_grad, states[0], states[1], states[2])
```

```python
import functools
import jax
import jax.numpy as jnp
from jax import lax
from jax.experimental import pallas as pl
from jax.experimental.pallas import tpu as pltpu
from jax.sharding import PartitionSpec as P

BF = jnp.bfloat16
F32 = jnp.float32
VMEM = 48 * 1024 * 1024
TILE = 512


def row_parts(rows, first, cap):
    per = 4 * cap
    r = lax.broadcasted_iota(jnp.int32, (rows, 128), 0) + first
    e = r // per
    q = r - e * per
    h = q // (2 * cap)
    q = q - h * (2 * cap)
    a = q // cap
    s = q - a * cap
    return e * cap + s, h, a


def dispatch_kernel(cap, slot_ref, prob_ref, t0, t1, c0, c1, out_ref, low, high, scale):
    rows = out_ref.shape[0]

    @pl.when(pl.program_id(0) == 0)
    def _():
        ident, h, a = row_parts(rows, 0, cap)
        hit0 = ident == slot_ref[0:1, :]
        hit1 = ident == slot_ref[1:2, :]
        hit = hit0 | hit1
        prob = jnp.where(hit0, prob_ref[0:1, :], 0.0) + jnp.where(hit1, prob_ref[1:2, :], 0.0)
        prob = jnp.sum(prob, axis=1, keepdims=True)
        scale[...] = jnp.where(a == 0, 1.0, prob)
        for ref, half in ((low, 0), (high, 1)):
            for kind in (0, 1):
                keep = hit & (h == half) & (a == kind)
                ref[:, kind * 128 : (kind + 1) * 128] = jnp.where(keep, 1.0, 0.0).astype(BF)

    x0 = jnp.concatenate([t0[...], c0[...]], axis=0)
    x1 = jnp.concatenate([t1[...], c1[...]], axis=0)
    step = rows // 4
    for i in range(4):
        part = slice(i * step, (i + 1) * step)
        acc = jnp.dot(low[part, :], x0, preferred_element_type=F32)
        acc = acc + jnp.dot(high[part, :], x1, preferred_element_type=F32)
        out_ref[part, :] = (acc * scale[part, 0:1]).astype(BF)


def dispatch(slots, probs, tokens, cotangent, experts, cap):
    tok, width = tokens.shape
    half = width // 2
    tiles = half // TILE
    rows = experts * cap * 4
    small = pl.BlockSpec((2, tok), lambda i: (0, 0))
    left = pl.BlockSpec((tok, TILE), lambda i: (0, i))
    right = pl.BlockSpec((tok, TILE), lambda i: (0, i + tiles))
    return pl.pallas_call(
        functools.partial(dispatch_kernel, cap),
        grid=(tiles,),
        in_specs=[small, small, left, right, left, right],
        out_specs=pl.BlockSpec((rows, TILE), lambda i: (0, i)),
        out_shape=jax.ShapeDtypeStruct((rows, half), BF),
        scratch_shapes=[
            pltpu.VMEM((rows, 2 * tok), BF),
            pltpu.VMEM((rows, 2 * tok), BF),
            pltpu.VMEM((rows, 128), F32),
        ],
        compiler_params=pltpu.CompilerParams(vmem_limit_bytes=VMEM),
        cost_estimate=pl.CostEstimate(
            flops=2 * rows * 2 * tok * width, bytes_accessed=16 * 1024 * 1024, transcendentals=0
        ),
        name="dispatch",
    )(slots, probs, tokens, tokens, cotangent, cotangent)


def order_matrix(group, cap, inverse):
    n = group * cap * 4
    i = lax.broadcasted_iota(jnp.int32, (n, n), 1 if inverse else 0)
    j = lax.broadcasted_iota(jnp.int32, (n, n), 0 if inverse else 1)
    hk = i // (group * cap)
    rest = i - hk * (group * cap)
    src = rest // cap
    slot = rest - src * cap
    return jnp.where(src * (4 * cap) + hk * cap + slot == j, 1.0, 0.0).astype(BF)


def expert_kernel(
    cap, group, tiles, rank_ref, recv_ref, w_ref, out_ref, mine_ref, theirs_ref,
    rows_x, rows_c, front, down, inner, pre, fore, back
):
    i = pl.program_id(0)
    n = group * cap
    span = 4 * n
    sets = recv_ref.shape[0] // span
    hidden = inner.shape[1]

    @pl.when(i == 0)
    def _():
        fore[...] = order_matrix(group, cap, False)
        back[...] = order_matrix(group, cap, True)
        front[...] = jnp.zeros_like(front)
        down[...] = jnp.zeros_like(down)

    @pl.when(i < tiles)
    def _():
        for g in range(sets):
            got = jnp.dot(
                fore[...], recv_ref[g * span : (g + 1) * span, :], preferred_element_type=F32
            ).astype(BF)
            at = slice(g * n, (g + 1) * n)
            for h in range(2):
                rows_x[i, h, at, :] = got[2 * h * n : (2 * h + 1) * n]
                rows_c[i, h, at, :] = got[(2 * h + 1) * n : (2 * h + 2) * n]
        for h in range(2):
            front[...] += jnp.dot(
                rows_x[i, h], w_ref[h, :, : 2 * hidden], preferred_element_type=F32
            )
            down[...] += jnp.dot(
                rows_c[i, h], w_ref[h, :, 2 * hidden :], preferred_element_type=F32
            )

    @pl.when(i == tiles - 1)
    def _():
        gate = front[:, :hidden]
        up = front[:, hidden:]
        sig = jax.nn.sigmoid(gate)
        active = gate * sig
        inner[...] = (active * up).astype(BF)
        grad = down[...]
        slope = sig * (1.0 + gate * (1.0 - sig))
        pre[:, :hidden] = (grad * up * slope).astype(BF)
        pre[:, hidden:] = (grad * active).astype(BF)

    @pl.when(i >= tiles)
    def _():
        c = i - tiles
        contract = (((1,), (1,)), ((), ()))
        lead = (((0,), (0,)), ((), ()))
        made = []
        for h in range(2):
            made.append(
                lax.dot_general(
                    inner[...], w_ref[h, :, 2 * hidden :], contract, preferred_element_type=F32
                ).astype(BF)
            )
            made.append(
                lax.dot_general(
                    pre[...], w_ref[h, :, : 2 * hidden], contract, preferred_element_type=F32
                ).astype(BF)
            )
        for g in range(sets):
            stack = jnp.concatenate([m[g * n : (g + 1) * n] for m in made], axis=0)
            out_ref[g * span : (g + 1) * span, :] = jnp.dot(
                back[...], stack, preferred_element_type=F32
            ).astype(BF)
        parts = []
        for h in range(2):
            parts.append(
                (
                    lax.dot_general(rows_x[c, h], pre[...], lead, preferred_element_type=F32),
                    lax.dot_general(rows_c[c, h], inner[...], lead, preferred_element_type=F32),
                )
            )
        first = rank_ref[0] == 0
        for k, at in ((0, slice(0, 2 * hidden)), (1, slice(2 * hidden, 3 * hidden))):
            mine_ref[:, at] = jnp.where(first, parts[0][k], parts[1][k]).astype(BF)
            theirs_ref[:, at] = jnp.where(first, parts[1][k], parts[0][k]).astype(BF)


def expert_call(rank, recv, weight, cap):
    total, half = recv.shape
    columns = weight.shape[1]
    hidden = columns // 3
    tiles = half // TILE
    rows = total // 4
    group = 8
    n = group * cap * 4
    late = lambda i: jnp.maximum(i - tiles, 0)
    return pl.pallas_call(
        functools.partial(expert_kernel, cap, group, tiles),
        grid=(2 * tiles,),
        in_specs=[
            pl.BlockSpec(memory_space=pltpu.SMEM),
            pl.BlockSpec((total, TILE), lambda i: (0, jnp.minimum(i, tiles - 1))),
            pl.BlockSpec((2, TILE, columns), lambda i: (0, lax.rem(i, tiles), 0)),
        ],
        out_specs=[
            pl.BlockSpec((total, TILE), lambda i: (0, late(i))),
            pl.BlockSpec((TILE, columns), lambda i: (late(i), 0)),
            pl.BlockSpec((TILE, columns), lambda i: (late(i), 0)),
        ],
        out_shape=[
            jax.ShapeDtypeStruct((total, half), BF),
            jax.ShapeDtypeStruct((half, columns), BF),
            jax.ShapeDtypeStruct((half, columns), BF),
        ],
        scratch_shapes=[
            pltpu.VMEM((tiles, 2, rows, TILE), BF),
            pltpu.VMEM((tiles, 2, rows, TILE), BF),
            pltpu.VMEM((rows, 2 * hidden), F32),
            pltpu.VMEM((rows, hidden), F32),
            pltpu.VMEM((rows, hidden), BF),
            pltpu.VMEM((rows, 2 * hidden), BF),
            pltpu.VMEM((n, n), BF),
            pltpu.VMEM((n, n), BF),
        ],
        compiler_params=pltpu.CompilerParams(vmem_limit_bytes=VMEM),
        cost_estimate=pl.CostEstimate(
            flops=10 * 10**9, bytes_accessed=34 * 1024 * 1024, transcendentals=rows * hidden
        ),
        name="expert_pass",
    )(rank, recv, weight.reshape(2, half, columns))


def combine_kernel(cap, tiles, slot_ref, prob_ref, back_ref, mixed_ref, grad_ref, pick):
    total = back_ref.shape[0]
    tok = mixed_ref.shape[0]
    i = pl.program_id(0)

    @pl.when(i == 0)
    def _():
        per = 4 * cap
        r = lax.broadcasted_iota(jnp.int32, (tok, total), 1)
        e = r // per
        q = r - e * per
        h = q // (2 * cap)
        q = q - h * (2 * cap)
        a = q // cap
        ident = e * cap + q - a * cap
        hit0 = ident == slot_ref[:, 0:1]
        hit1 = ident == slot_ref[:, 1:2]
        for half in range(2):
            out = (h == half) & (a == 0)
            pick[3 * half] = jnp.where(hit0 & out, 1.0, 0.0).astype(BF)
            pick[3 * half + 1] = jnp.where(hit1 & out, 1.0, 0.0).astype(BF)
            pick[3 * half + 2] = jnp.where(
                (hit0 | hit1) & (h == half) & (a == 1), 1.0, 0.0
            ).astype(BF)

    for half in range(2):
        at = pl.ds(pl.multiple_of(half * tiles * TILE + i * TILE, TILE), TILE)
        block = back_ref[...]
        one = jnp.dot(pick[3 * half], block, preferred_element_type=F32)
        two = jnp.dot(pick[3 * half + 1], block, preferred_element_type=F32)
        both = jnp.dot(pick[3 * half + 2], block, preferred_element_type=F32)
        mixed_ref[:, at] = (one * prob_ref[:, 0:1] + two * prob_ref[:, 1:2]).astype(BF)
        grad_ref[:, at] = both.astype(BF)


def combine(slots, probs, back, cap):
    total, half = back.shape
    tok = slots.shape[0]
    tiles = half // TILE
    whole = pl.BlockSpec((tok, 2 * half), lambda i: (0, 0))
    small = pl.BlockSpec((tok, 2), lambda i: (0, 0))
    shape = jax.ShapeDtypeStruct((tok, 2 * half), BF)
    return pl.pallas_call(
        functools.partial(combine_kernel, cap, tiles),
        grid=(tiles,),
        in_specs=[small, small, pl.BlockSpec((total, TILE), lambda i: (0, i))],
        out_specs=[whole, whole],
        out_shape=[shape, shape],
        scratch_shapes=[pltpu.VMEM((6, tok, total), BF)],
        compiler_params=pltpu.CompilerParams(vmem_limit_bytes=VMEM),
        cost_estimate=pl.CostEstimate(
            flops=2 * 6 * tok * total * half, bytes_accessed=13 * 1024 * 1024, transcendentals=0
        ),
        name="combine",
    )(slots, probs, back)


def moments_kernel(piece, mine, other, first, second, out):
    grad = mine[...].astype(F32) + other[...].astype(F32)
    m = (0.9 * first[...].astype(F32) + 0.1 * grad).astype(BF)
    v = (0.95 * second[...].astype(F32) + 0.05 * grad * grad).astype(BF)
    for j in range(mine.shape[0] // piece):
        out[2 * j * piece : (2 * j + 1) * piece, :] = m[j * piece : (j + 1) * piece]
        out[(2 * j + 1) * piece : (2 * j + 2) * piece, :] = v[j * piece : (j + 1) * piece]


def moments(mine, other, first, second, piece):
    rows, columns = mine.shape
    block = 8 * piece
    spec = pl.BlockSpec((block, columns), lambda i: (i, 0))
    return pl.pallas_call(
        functools.partial(moments_kernel, piece),
        grid=(rows // block,),
        in_specs=[spec] * 4,
        out_specs=pl.BlockSpec((2 * block, columns), lambda i: (i, 0)),
        out_shape=jax.ShapeDtypeStruct((2 * rows, columns), BF),
        compiler_params=pltpu.CompilerParams(vmem_limit_bytes=VMEM),
        cost_estimate=pl.CostEstimate(
            flops=10 * rows * columns, bytes_accessed=12 * rows * columns, transcendentals=0
        ),
        name="moments",
    )(mine, other, first, second)


def step_kernel(piece, both, weight, m_out, v_out, step_out):
    for j in range(weight.shape[0] // piece):
        at = slice(j * piece, (j + 1) * piece)
        m = both[2 * j * piece : (2 * j + 1) * piece, :]
        v = both[(2 * j + 1) * piece : (2 * j + 2) * piece, :]
        m_out[at, :] = m
        v_out[at, :] = v
        step = m.astype(F32) / (jnp.sqrt(v.astype(F32)) + 1e-08)
        step_out[at, :] = (step + 0.1 * weight[at, :].astype(F32)).astype(BF)


def final_step(both, weight, piece):
    rows, columns = weight.shape
    block = 8 * piece
    spec = pl.BlockSpec((block, columns), lambda i: (i, 0))
    shape = jax.ShapeDtypeStruct((rows, columns), BF)
    return pl.pallas_call(
        functools.partial(step_kernel, piece),
        grid=(rows // block,),
        in_specs=[pl.BlockSpec((2 * block, columns), lambda i: (i, 0)), spec],
        out_specs=[spec] * 3,
        out_shape=[shape] * 3,
        compiler_params=pltpu.CompilerParams(vmem_limit_bytes=VMEM),
        cost_estimate=pl.CostEstimate(
            flops=10 * rows * columns, bytes_accessed=12 * rows * columns, transcendentals=0
        ),
        name="final_step",
    )(both, weight)


def swap(array):
    return lax.all_to_all(array, "expert", split_axis=0, concat_axis=0, tiled=True)


def reorder(array, inverse):
    count = inverse.shape[0]
    pieces = array.reshape(count, array.shape[0] // count, array.shape[1])
    return jnp.take(pieces, inverse, axis=0, mode="clip").reshape(array.shape)


def local(tokens, cotangent, gate_probs, routes, placement, weights, first_moment, second_moment):
    experts = lax.axis_size("expert")
    tok, width = tokens.shape
    top = routes.shape[1]
    cap = max(2, (3 * tok * top + 2 * experts - 1) // (2 * experts))
    ids = routes.reshape(-1)
    labels = jnp.arange(experts, dtype=jnp.int32)
    onehot = (ids[:, None] == labels[None, :]).astype(jnp.int32)
    earlier = jnp.sum((jnp.cumsum(onehot, axis=0) - onehot) * onehot, axis=1)
    slots = (ids * cap + earlier).reshape(tok, top)
    inverse = jnp.sum(
        labels[None, :] * (placement[None, :] == labels[:, None]).astype(jnp.int32), axis=1
    )
    rank = lax.axis_index("dp")
    weight = weights[0]
    rows = weight.shape[0] // 2
    piece = rows // experts

    send = dispatch(slots.T, gate_probs.T, tokens, cotangent, experts, cap)
    recv = swap(send)
    half = lax.dynamic_slice_in_dim(weight, rank * rows, rows, 0)
    spread_w = swap(half)
    result, mine, theirs = expert_call(rank.reshape(1).astype(jnp.int32), recv, weight, cap)
    other = lax.ppermute(theirs, "dp", [(0, 1), (1, 0)])
    back = swap(result)
    mixed, token_grad = combine(slots, gate_probs, back, cap)
    state = moments(mine, other, first_moment[0], second_moment[0], piece)
    spread_state = swap(state)
    moved_w = swap(reorder(spread_w, inverse))
    moved_state = swap(reorder(spread_state, inverse))
    m, v, step = final_step(moved_state, moved_w, piece)
    return (mixed, token_grad, m[None], v[None], step[None])


def solution(mesh):
    in_specs = (
        P(("expert", "dp"), None),
        P(("expert", "dp"), None),
        P(("expert", "dp"), None),
        P(("expert", "dp"), None),
        P(),
        P("expert", None, None),
        P("expert", "dp", None),
        P("expert", "dp", None),
    )
    out_specs = (
        P(("expert", "dp"), None),
        P(("expert", "dp"), None),
        P("expert", "dp", None),
        P("expert", "dp", None),
        P("expert", "dp", None),
    )
    return jax.shard_map(local, mesh=mesh, in_specs=in_specs, out_specs=out_specs, check_vma=False)
```

```python
import functools
import jax
import jax.numpy as jnp
from jax import lax
from jax.experimental import pallas as pl
from jax.experimental.pallas import tpu as pltpu
from jax.sharding import PartitionSpec as P

BF = jnp.bfloat16
F32 = jnp.float32
VMEM = 48 * 1024 * 1024
TILE = 512


def row_parts(rows, first, cap):
    per = 4 * cap
    r = lax.broadcasted_iota(jnp.int32, (rows, 128), 0) + first
    e = r // per
    q = r - e * per
    h = q // (2 * cap)
    q = q - h * (2 * cap)
    a = q // cap
    s = q - a * cap
    return e * cap + s, h, a


def dispatch_kernel(cap, slot_ref, prob_ref, t0, t1, c0, c1, out_ref, low, high, scale):
    rows = out_ref.shape[0]

    @pl.when((pl.program_id(0) == 0) & (pl.program_id(1) == 0))
    def _():
        ident, h, a = row_parts(rows, 0, cap)
        hit0 = ident == slot_ref[0:1, :]
        hit1 = ident == slot_ref[1:2, :]
        hit = hit0 | hit1
        prob = jnp.where(hit0, prob_ref[0:1, :], 0.0) + jnp.where(hit1, prob_ref[1:2, :], 0.0)
        prob = jnp.sum(prob, axis=1, keepdims=True)
        scale[...] = jnp.where(a == 0, 1.0, prob)
        for ref, half in ((low, 0), (high, 1)):
            for kind in (0, 1):
                keep = hit & (h == half) & (a == kind)
                ref[:, kind * 128 : (kind + 1) * 128] = jnp.where(keep, 1.0, 0.0).astype(BF)

    x0 = jnp.concatenate([t0[...], c0[...]], axis=0)
    x1 = jnp.concatenate([t1[...], c1[...]], axis=0)
    step = rows // 4
    for i in range(4):
        part = slice(i * step, (i + 1) * step)
        acc = jnp.dot(low[part, :], x0, preferred_element_type=F32)
        acc = acc + jnp.dot(high[part, :], x1, preferred_element_type=F32)
        out_ref[part, :] = (acc * scale[part, 0:1]).astype(BF)


def dispatch(slots, probs, tokens, cotangent, experts, cap):
    tok, width = tokens.shape
    half = width // 4
    tiles = half // TILE
    rows = experts * cap * 4
    small = pl.BlockSpec((2, tok), lambda r, i: (0, 0))
    left = pl.BlockSpec((tok, TILE), lambda r, i: (0, 2 * r * tiles + i))
    right = pl.BlockSpec((tok, TILE), lambda r, i: (0, (2 * r + 1) * tiles + i))
    return pl.pallas_call(
        functools.partial(dispatch_kernel, cap),
        grid=(2, tiles),
        in_specs=[small, small, left, right, left, right],
        out_specs=pl.BlockSpec((rows, TILE), lambda r, i: (r, i)),
        out_shape=jax.ShapeDtypeStruct((2 * rows, half), BF),
        scratch_shapes=[
            pltpu.VMEM((rows, 2 * tok), BF),
            pltpu.VMEM((rows, 2 * tok), BF),
            pltpu.VMEM((rows, 128), F32),
        ],
        compiler_params=pltpu.CompilerParams(vmem_limit_bytes=VMEM),
        cost_estimate=pl.CostEstimate(
            flops=2 * rows * 2 * tok * width, bytes_accessed=16 * 1024 * 1024, transcendentals=0
        ),
        name="dispatch",
    )(slots, probs, tokens, tokens, cotangent, cotangent)


def order_matrix(group, cap, inverse):
    n = group * cap * 4
    i = lax.broadcasted_iota(jnp.int32, (n, n), 1 if inverse else 0)
    j = lax.broadcasted_iota(jnp.int32, (n, n), 0 if inverse else 1)
    hk = i // (group * cap)
    rest = i - hk * (group * cap)
    src = rest // cap
    slot = rest - src * cap
    return jnp.where(src * (4 * cap) + hk * cap + slot == j, 1.0, 0.0).astype(BF)


def front_kernel(cap, group, rank_ref, recv_ref, w_ref, x_ref, c_ref, sum_ref, send_ref, fore):
    i = pl.program_id(0)
    n = group * cap
    span = 4 * n
    sets = recv_ref.shape[0] // span
    hidden = sum_ref.shape[1] // 3

    @pl.when(i == 0)
    def _():
        fore[...] = order_matrix(group, cap, False)
        sum_ref[...] = jnp.zeros_like(sum_ref)

    for g in range(sets):
        got = jnp.dot(
            fore[...], recv_ref[g * span : (g + 1) * span, :], preferred_element_type=F32
        ).astype(BF)
        at = slice(g * n, (g + 1) * n)
        for h in range(2):
            x_ref[h, at, :] = got[2 * h * n : (2 * h + 1) * n]
            c_ref[h, at, :] = got[(2 * h + 1) * n : (2 * h + 2) * n]
    for h in range(2):
        sum_ref[:, : 2 * hidden] += jnp.dot(
            x_ref[h], w_ref[0, h, :, : 2 * hidden], preferred_element_type=F32
        )
        sum_ref[:, 2 * hidden :] += jnp.dot(
            c_ref[h], w_ref[0, h, :, 2 * hidden :], preferred_element_type=F32
        )

    @pl.when(i == pl.num_programs(0) - 1)
    def _():
        send_ref[...] = sum_ref[...].astype(BF)


GROUP = 8


def front_call(rank, recv, weight, cap):
    total, half = recv.shape
    columns = weight.shape[-1]
    tiles = half // TILE
    rows = total // 4
    n = GROUP * cap * 4
    held = pl.BlockSpec((2, rows, TILE), lambda i, r: (0, 0, i))
    small = pl.BlockSpec((rows, columns), lambda i, r: (0, 0))
    return pl.pallas_call(
        functools.partial(front_kernel, cap, GROUP),
        grid_spec=pltpu.PrefetchScalarGridSpec(
            num_scalar_prefetch=1,
            grid=(tiles,),
            in_specs=[
                pl.BlockSpec((total, TILE), lambda i, r: (0, i)),
                pl.BlockSpec((1, 2, TILE, columns), lambda i, r: (r[0], 0, i, 0)),
            ],
            out_specs=[held, held, small, small],
            scratch_shapes=[pltpu.VMEM((n, n), BF)],
        ),
        out_shape=[
            jax.ShapeDtypeStruct((2, rows, half), BF),
            jax.ShapeDtypeStruct((2, rows, half), BF),
            jax.ShapeDtypeStruct((rows, columns), F32),
            jax.ShapeDtypeStruct((rows, columns), BF),
        ],
        compiler_params=pltpu.CompilerParams(vmem_limit_bytes=VMEM),
        cost_estimate=pl.CostEstimate(
            flops=5 * 10**9, bytes_accessed=22 * 1024 * 1024, transcendentals=0
        ),
        name="expert_front",
    )(rank, recv, weight.reshape(2, 2, half, columns))


def rear_kernel(
    cap, group, piece, rank_ref, x_ref, c_ref, own_ref, other_ref, w_ref, first_ref, second_ref,
    out_ref, state_ref, inner, pre, back
):
    i = pl.program_id(0)
    n = group * cap
    span = 4 * n
    sets = out_ref.shape[0] // span
    hidden = inner.shape[1]

    @pl.when(i == 0)
    def _():
        back[...] = order_matrix(group, cap, True)
        total = own_ref[...] + other_ref[...].astype(F32)
        gate = total[:, :hidden]
        up = total[:, hidden : 2 * hidden]
        grad = total[:, 2 * hidden :]
        sig = jax.nn.sigmoid(gate)
        active = gate * sig
        inner[...] = (active * up).astype(BF)
        slope = sig * (1.0 + gate * (1.0 - sig))
        pre[:, :hidden] = (grad * up * slope).astype(BF)
        pre[:, hidden:] = (grad * active).astype(BF)

    contract = (((1,), (1,)), ((), ()))
    lead = (((0,), (0,)), ((), ()))
    made = []
    for h in range(2):
        made.append(
            lax.dot_general(
                inner[...], w_ref[0, h, :, 2 * hidden :], contract, preferred_element_type=F32
            ).astype(BF)
        )
        made.append(
            lax.dot_general(
                pre[...], w_ref[0, h, :, : 2 * hidden], contract, preferred_element_type=F32
            ).astype(BF)
        )
    for g in range(sets):
        stack = jnp.concatenate([m[g * n : (g + 1) * n] for m in made], axis=0)
        out_ref[g * span : (g + 1) * span, :] = jnp.dot(
            back[...], stack, preferred_element_type=F32
        ).astype(BF)
    for h in range(2):
        for source, factor, at in (
            (x_ref, pre, slice(0, 2 * hidden)),
            (c_ref, inner, slice(2 * hidden, 3 * hidden)),
        ):
            grad = lax.dot_general(source[h], factor[...], lead, preferred_element_type=F32)
            m = (0.9 * first_ref[h, :, at].astype(F32) + 0.1 * grad).astype(BF)
            v = (0.95 * second_ref[h, :, at].astype(F32) + 0.05 * grad * grad).astype(BF)
            for j in range(grad.shape[0] // piece):
                state_ref[h, j, :piece, at] = m[j * piece : (j + 1) * piece]
                state_ref[h, j, piece:, at] = v[j * piece : (j + 1) * piece]


def rear_call(rank, x, c, own, other, weight, first, second, cap, piece):
    half = x.shape[2]
    rows, columns = own.shape
    hidden = columns // 3
    tile = 8 * piece
    tiles = half // tile
    total = 4 * rows
    n = GROUP * cap * 4
    held = pl.BlockSpec((2, rows, tile), lambda i, r: (0, 0, i))
    small = pl.BlockSpec((rows, columns), lambda i, r: (0, 0))
    moment = pl.BlockSpec((2, tile, columns), lambda i, r: (0, i, 0))
    return pl.pallas_call(
        functools.partial(rear_kernel, cap, GROUP, piece),
        grid_spec=pltpu.PrefetchScalarGridSpec(
            num_scalar_prefetch=1,
            grid=(tiles,),
            in_specs=[
                held,
                held,
                small,
                small,
                pl.BlockSpec((1, 2, tile, columns), lambda i, r: (r[0], 0, i, 0)),
                moment,
                moment,
            ],
            out_specs=[
                pl.BlockSpec((total, tile), lambda i, r: (0, i)),
                pl.BlockSpec((2, 8, 2 * piece, columns), lambda i, r: (0, i, 0, 0)),
            ],
            scratch_shapes=[
                pltpu.VMEM((rows, hidden), BF),
                pltpu.VMEM((rows, 2 * hidden), BF),
                pltpu.VMEM((n, n), BF),
            ],
        ),
        out_shape=[
            jax.ShapeDtypeStruct((total, half), BF),
            jax.ShapeDtypeStruct((2, half // piece, 2 * piece, columns), BF),
        ],
        compiler_params=pltpu.CompilerParams(vmem_limit_bytes=VMEM),
        cost_estimate=pl.CostEstimate(
            flops=7 * 10**9, bytes_accessed=34 * 1024 * 1024, transcendentals=rows * hidden
        ),
        name="expert_rear",
    )(
        rank, x, c, own, other, weight.reshape(2, 2, half, columns),
        first.reshape(2, half, columns), second.reshape(2, half, columns),
    )


def combine_kernel(cap, tiles, slot_ref, prob_ref, back_ref, mixed_ref, grad_ref, pick):
    total = back_ref.shape[0]
    tok = mixed_ref.shape[0]
    part = pl.program_id(0)
    i = pl.program_id(1)

    @pl.when((part == 0) & (i == 0))
    def _():
        per = 4 * cap
        r = lax.broadcasted_iota(jnp.int32, (tok, total), 1)
        e = r // per
        q = r - e * per
        h = q // (2 * cap)
        q = q - h * (2 * cap)
        a = q // cap
        ident = e * cap + q - a * cap
        hit0 = ident == slot_ref[:, 0:1]
        hit1 = ident == slot_ref[:, 1:2]
        for half in range(2):
            out = (h == half) & (a == 0)
            pick[3 * half] = jnp.where(hit0 & out, 1.0, 0.0).astype(BF)
            pick[3 * half + 1] = jnp.where(hit1 & out, 1.0, 0.0).astype(BF)
            pick[3 * half + 2] = jnp.where(
                (hit0 | hit1) & (h == half) & (a == 1), 1.0, 0.0
            ).astype(BF)

    for half in range(2):
        at = pl.ds(pl.multiple_of(((2 * part + half) * tiles + i) * TILE, TILE), TILE)
        block = back_ref[...]
        one = jnp.dot(pick[3 * half], block, preferred_element_type=F32)
        two = jnp.dot(pick[3 * half + 1], block, preferred_element_type=F32)
        both = jnp.dot(pick[3 * half + 2], block, preferred_element_type=F32)
        mixed_ref[:, at] = (one * prob_ref[:, 0:1] + two * prob_ref[:, 1:2]).astype(BF)
        grad_ref[:, at] = both.astype(BF)


def combine(slots, probs, back, cap):
    total, half = back.shape
    total = total // 2
    tok = slots.shape[0]
    tiles = half // TILE
    whole = pl.BlockSpec((tok, 4 * half), lambda r, i: (0, 0))
    small = pl.BlockSpec((tok, 2), lambda r, i: (0, 0))
    shape = jax.ShapeDtypeStruct((tok, 4 * half), BF)
    return pl.pallas_call(
        functools.partial(combine_kernel, cap, tiles),
        grid=(2, tiles),
        in_specs=[small, small, pl.BlockSpec((total, TILE), lambda r, i: (r, i))],
        out_specs=[whole, whole],
        out_shape=[shape, shape],
        scratch_shapes=[pltpu.VMEM((6, tok, total), BF)],
        compiler_params=pltpu.CompilerParams(vmem_limit_bytes=VMEM),
        cost_estimate=pl.CostEstimate(
            flops=2 * 12 * tok * total * half, bytes_accessed=13 * 1024 * 1024, transcendentals=0
        ),
        name="combine",
    )(slots, probs, back)


def step_kernel(piece, both, weight, m_out, v_out, step_out):
    for j in range(weight.shape[0] // piece):
        at = slice(j * piece, (j + 1) * piece)
        m = both[2 * j * piece : (2 * j + 1) * piece, :]
        v = both[(2 * j + 1) * piece : (2 * j + 2) * piece, :]
        m_out[at, :] = m
        v_out[at, :] = v
        step = m.astype(F32) / (jnp.sqrt(v.astype(F32)) + 1e-08)
        step_out[at, :] = (step + 0.1 * weight[at, :].astype(F32)).astype(BF)


def final_step(both, weight, piece):
    rows, columns = weight.shape
    block = 8 * piece
    spec = pl.BlockSpec((block, columns), lambda i: (i, 0))
    shape = jax.ShapeDtypeStruct((rows, columns), BF)
    return pl.pallas_call(
        functools.partial(step_kernel, piece),
        grid=(rows // block,),
        in_specs=[pl.BlockSpec((2 * block, columns), lambda i: (i, 0)), spec],
        out_specs=[spec] * 3,
        out_shape=[shape] * 3,
        compiler_params=pltpu.CompilerParams(vmem_limit_bytes=VMEM),
        cost_estimate=pl.CostEstimate(
            flops=10 * rows * columns, bytes_accessed=12 * rows * columns, transcendentals=0
        ),
        name="final_step",
    )(both, weight)


def swap(array, axes="expert"):
    return lax.all_to_all(array, axes, split_axis=0, concat_axis=0, tiled=True)


def reorder(array, inverse):
    count = inverse.shape[0]
    pieces = array.reshape(count, array.shape[0] // count, array.shape[1])
    return jnp.take(pieces, inverse, axis=0, mode="clip").reshape(array.shape)


def local(tokens, cotangent, gate_probs, routes, placement, weights, first_moment, second_moment):
    experts = lax.axis_size("expert")
    tok, width = tokens.shape
    top = routes.shape[1]
    cap = max(2, (3 * tok * top + 2 * experts - 1) // (2 * experts))
    ids = routes.reshape(-1)
    labels = jnp.arange(experts, dtype=jnp.int32)
    onehot = (ids[:, None] == labels[None, :]).astype(jnp.int32)
    earlier = jnp.sum((jnp.cumsum(onehot, axis=0) - onehot) * onehot, axis=1)
    slots = (ids * cap + earlier).reshape(tok, top)
    inverse = jnp.sum(
        labels[None, :] * (placement[None, :] == labels[:, None]).astype(jnp.int32), axis=1
    )
    rank = lax.axis_index("dp")
    weight = weights[0]
    rows = weight.shape[0] // 2
    piece = rows // experts
    columns = weight.shape[1]
    both = ("dp", "expert")
    together = lax.optimization_barrier

    spread_w = swap(lax.dynamic_slice_in_dim(weight, rank * rows, rows, 0))
    send = dispatch(slots.T, gate_probs.T, tokens, cotangent, experts, cap)
    send, spread_w = together((send, spread_w))
    recv = swap(send, both)
    ready_w, recv = together((reorder(spread_w, inverse), recv))
    moved_w = swap(ready_w)
    place = rank.reshape(1).astype(jnp.int32)
    x, c, own, out = front_call(place, recv, weight, cap)
    other = lax.ppermute(out, "dp", [(0, 1), (1, 0)])
    result, state = rear_call(
        place, x, c, own, other, weight, first_moment[0], second_moment[0], cap, piece
    )
    state, moved_w = together((state, moved_w))
    spread_state = swap(state.reshape(2 * rows, columns))
    result, spread_state = together((result, spread_state))
    back = swap(result, both)
    ready_state, back = together((reorder(spread_state, inverse), back))
    moved_state = swap(ready_state)
    mixed, token_grad = combine(slots, gate_probs, back, cap)
    m, v, step = final_step(moved_state, moved_w, piece)
    return (mixed, token_grad, m[None], v[None], step[None])


def solution(mesh):
    in_specs = (
        P(("expert", "dp"), None),
        P(("expert", "dp"), None),
        P(("expert", "dp"), None),
        P(("expert", "dp"), None),
        P(),
        P("expert", None, None),
        P("expert", "dp", None),
        P("expert", "dp", None),
    )
    out_specs = (
        P(("expert", "dp"), None),
        P(("expert", "dp"), None),
        P("expert", "dp", None),
        P("expert", "dp", None),
        P("expert", "dp", None),
    )
    return jax.shard_map(local, mesh=mesh, in_specs=in_specs, out_specs=out_specs, check_vma=False)
```

```python
import functools
import jax
import jax.numpy as jnp
from jax import lax
from jax.experimental import pallas as pl
from jax.experimental.pallas import tpu as pltpu
from jax.sharding import PartitionSpec as P

BF = jnp.bfloat16
F32 = jnp.float32
MIB = 1024 * 1024
DISPATCH_VMEM, FRONT_VMEM, REAR_VMEM, COMBINE_VMEM = 56 * MIB, 48 * MIB, 56 * MIB, 40 * MIB
TILE = 512


def row_parts(shape, axis, cap):
    per = 4 * cap
    r = lax.broadcasted_iota(jnp.int32, shape, axis)
    e = r // per
    q = r - e * per
    h = q // (2 * cap)
    q = q - h * (2 * cap)
    a = q // cap
    return e * cap + q - a * cap, h, a


def dispatch_kernel(cap, experts, route_ref, prob_ref, t0, t1, c0, c1, out_ref, low, high, scale):
    per = 4 * cap
    rows = experts * per

    @pl.when((pl.program_id(0) == 0) & (pl.program_id(1) == 0))
    def _():
        tok = route_ref.shape[1]
        label = lax.broadcasted_iota(jnp.int32, (experts, tok), 0)
        one0 = jnp.where(label == route_ref[0:1, :], 1.0, 0.0)
        one1 = jnp.where(label == route_ref[1:2, :], 1.0, 0.0)
        before = lax.broadcasted_iota(jnp.int32, (tok, tok), 0) < lax.broadcasted_iota(
            jnp.int32, (tok, tok), 1
        )
        count = jnp.dot(
            (one0 + one1).astype(BF),
            jnp.where(before, 1.0, 0.0).astype(BF),
            preferred_element_type=F32,
        )
        earlier0 = jnp.sum(one0 * count, axis=0, keepdims=True).astype(jnp.int32)
        earlier1 = jnp.sum(one1 * count, axis=0, keepdims=True).astype(jnp.int32)
        ident, h, a = row_parts((rows, tok), 0, cap)
        hit0 = ident == route_ref[0:1, :] * cap + earlier0
        hit1 = ident == route_ref[1:2, :] * cap + earlier1
        hit = hit0 | hit1
        prob = jnp.where(hit0, prob_ref[0:1, :], 0.0) + jnp.where(hit1, prob_ref[1:2, :], 0.0)
        prob = jnp.sum(prob, axis=1, keepdims=True)
        scale[...] = jnp.where(a == 0, 1.0, prob)
        for ref, half in ((low, 0), (high, 1)):
            for kind in (0, 1):
                keep = hit & (h == half) & (a == kind)
                ref[:, kind * tok : (kind + 1) * tok] = jnp.where(keep, 1.0, 0.0).astype(BF)

    x0 = jnp.concatenate([t0[...], c0[...]], axis=0)
    x1 = jnp.concatenate([t1[...], c1[...]], axis=0)
    step = rows // 4
    for i in range(4):
        part = slice(i * step, (i + 1) * step)
        acc = jnp.dot(low[part, :], x0, preferred_element_type=F32)
        acc = acc + jnp.dot(high[part, :], x1, preferred_element_type=F32)
        acc = acc * scale[part, 0:1]
        for j in range(step // per):
            out_ref[i * (step // per) + j, 0] = acc[j * per : (j + 1) * per].astype(BF)


def dispatch(routes, probs, tokens, cotangent, experts, cap):
    tok, width = tokens.shape
    half = width // 4
    tiles = half // TILE
    per = 4 * cap
    rows = experts * per
    small = pl.BlockSpec((2, tok), lambda r, i: (0, 0))
    left = pl.BlockSpec((tok, TILE), lambda r, i: (0, 2 * r * tiles + i))
    right = pl.BlockSpec((tok, TILE), lambda r, i: (0, (2 * r + 1) * tiles + i))
    return pl.pallas_call(
        functools.partial(dispatch_kernel, cap, experts),
        grid=(2, tiles),
        in_specs=[small, small, left, right, left, right],
        out_specs=pl.BlockSpec((experts, 1, per, TILE), lambda r, i: (0, r, 0, i)),
        out_shape=jax.ShapeDtypeStruct((experts, 2, per, half), BF),
        scratch_shapes=[
            pltpu.VMEM((rows, 2 * tok), BF),
            pltpu.VMEM((rows, 2 * tok), BF),
            pltpu.VMEM((rows, 128), F32),
        ],
        compiler_params=pltpu.CompilerParams(vmem_limit_bytes=DISPATCH_VMEM),
        cost_estimate=pl.CostEstimate(
            flops=2 * rows * 2 * tok * width, bytes_accessed=16 * MIB, transcendentals=0
        ),
        name="dispatch",
    )(routes, probs, tokens, tokens, cotangent, cotangent)


def order_matrix(group, cap, inverse):
    n = group * cap * 4
    i = lax.broadcasted_iota(jnp.int32, (n, n), 1 if inverse else 0)
    j = lax.broadcasted_iota(jnp.int32, (n, n), 0 if inverse else 1)
    hk = i // (group * cap)
    rest = i - hk * (group * cap)
    src = rest // cap
    slot = rest - src * cap
    return jnp.where(src * (4 * cap) + hk * cap + slot == j, 1.0, 0.0).astype(BF)


def front_kernel(cap, group, rank_ref, recv_ref, w_ref, x_ref, c_ref, sum_ref, send_ref, fore):
    i = pl.program_id(0)
    n = group * cap
    span = 4 * n
    sets = recv_ref.shape[0] // span
    hidden = sum_ref.shape[1] // 3

    @pl.when(i == 0)
    def _():
        fore[...] = order_matrix(group, cap, False)
        sum_ref[...] = jnp.zeros_like(sum_ref)

    for g in range(sets):
        got = jnp.dot(
            fore[...], recv_ref[g * span : (g + 1) * span, :], preferred_element_type=F32
        ).astype(BF)
        at = slice(g * n, (g + 1) * n)
        for h in range(2):
            x_ref[h, at, :] = got[2 * h * n : (2 * h + 1) * n]
            c_ref[h, at, :] = got[(2 * h + 1) * n : (2 * h + 2) * n]
    for h in range(2):
        sum_ref[:, : 2 * hidden] += jnp.dot(
            x_ref[h], w_ref[0, h, :, : 2 * hidden], preferred_element_type=F32
        )
        sum_ref[:, 2 * hidden :] += jnp.dot(
            c_ref[h], w_ref[0, h, :, 2 * hidden :], preferred_element_type=F32
        )

    @pl.when(i == pl.num_programs(0) - 1)
    def _():
        send_ref[...] = sum_ref[...].astype(BF)


GROUP = 8


def front_call(rank, recv, weight, cap):
    total, half = recv.shape
    columns = weight.shape[-1]
    tiles = half // TILE
    rows = total // 4
    n = GROUP * cap * 4
    held = pl.BlockSpec((2, rows, TILE), lambda i, r: (0, 0, i))
    small = pl.BlockSpec((rows, columns), lambda i, r: (0, 0))
    return pl.pallas_call(
        functools.partial(front_kernel, cap, GROUP),
        grid_spec=pltpu.PrefetchScalarGridSpec(
            num_scalar_prefetch=1,
            grid=(tiles,),
            in_specs=[
                pl.BlockSpec((total, TILE), lambda i, r: (0, i)),
                pl.BlockSpec((1, 2, TILE, columns), lambda i, r: (r[0], 0, i, 0)),
            ],
            out_specs=[held, held, small, small],
            scratch_shapes=[pltpu.VMEM((n, n), BF)],
        ),
        out_shape=[
            jax.ShapeDtypeStruct((2, rows, half), BF),
            jax.ShapeDtypeStruct((2, rows, half), BF),
            jax.ShapeDtypeStruct((rows, columns), F32),
            jax.ShapeDtypeStruct((rows, columns), BF),
        ],
        compiler_params=pltpu.CompilerParams(vmem_limit_bytes=FRONT_VMEM),
        cost_estimate=pl.CostEstimate(
            flops=5 * 10**9, bytes_accessed=22 * 1024 * 1024, transcendentals=0
        ),
        name="expert_front",
    )(rank, recv, weight.reshape(2, 2, half, columns))


def rear_kernel(
    cap, group, piece, rank_ref, x_ref, c_ref, own_ref, other_ref, w_ref, first_ref, second_ref,
    out_ref, state_ref, inner, pre, back
):
    i = pl.program_id(0)
    n = group * cap
    span = 4 * n
    sets = out_ref.shape[0] // span
    hidden = inner.shape[1]

    @pl.when(i == 0)
    def _():
        back[...] = order_matrix(group, cap, True)
        total = own_ref[...] + other_ref[...].astype(F32)
        gate = total[:, :hidden]
        up = total[:, hidden : 2 * hidden]
        grad = total[:, 2 * hidden :]
        sig = jax.nn.sigmoid(gate)
        active = gate * sig
        inner[...] = (active * up).astype(BF)
        slope = sig * (1.0 + gate * (1.0 - sig))
        pre[:, :hidden] = (grad * up * slope).astype(BF)
        pre[:, hidden:] = (grad * active).astype(BF)

    contract = (((1,), (1,)), ((), ()))
    lead = (((0,), (0,)), ((), ()))
    made = []
    for h in range(2):
        made.append(
            lax.dot_general(
                inner[...], w_ref[0, h, :, 2 * hidden :], contract, preferred_element_type=F32
            ).astype(BF)
        )
        made.append(
            lax.dot_general(
                pre[...], w_ref[0, h, :, : 2 * hidden], contract, preferred_element_type=F32
            ).astype(BF)
        )
    for g in range(sets):
        stack = jnp.concatenate([m[g * n : (g + 1) * n] for m in made], axis=0)
        out_ref[g * span : (g + 1) * span, :] = jnp.dot(
            back[...], stack, preferred_element_type=F32
        ).astype(BF)
    for h in range(2):
        for source, factor, at in (
            (x_ref, pre, slice(0, 2 * hidden)),
            (c_ref, inner, slice(2 * hidden, 3 * hidden)),
        ):
            grad = lax.dot_general(source[h], factor[...], lead, preferred_element_type=F32)
            m = 0.9 * first_ref[h, :, at].astype(F32) + 0.1 * grad
            v = 0.95 * second_ref[h, :, at].astype(F32) + 0.05 * grad * grad
            step = m / (jnp.sqrt(v) + 1e-08) + 0.1 * w_ref[0, h, :, at].astype(F32)
            for k, value in enumerate((m, v, step)):
                value = value.astype(BF)
                for j in range(grad.shape[0] // piece):
                    state_ref[h, j, k * piece : (k + 1) * piece, at] = value[
                        j * piece : (j + 1) * piece
                    ]


def rear_call(rank, x, c, own, other, weight, first, second, cap, piece):
    half = x.shape[2]
    rows, columns = own.shape
    hidden = columns // 3
    tile = 8 * piece
    tiles = half // tile
    total = 4 * rows
    n = GROUP * cap * 4
    held = pl.BlockSpec((2, rows, tile), lambda i, r: (0, 0, i))
    small = pl.BlockSpec((rows, columns), lambda i, r: (0, 0))
    moment = pl.BlockSpec((2, tile, columns), lambda i, r: (0, i, 0))
    return pl.pallas_call(
        functools.partial(rear_kernel, cap, GROUP, piece),
        grid_spec=pltpu.PrefetchScalarGridSpec(
            num_scalar_prefetch=1,
            grid=(tiles,),
            in_specs=[
                held,
                held,
                small,
                small,
                pl.BlockSpec((1, 2, tile, columns), lambda i, r: (r[0], 0, i, 0)),
                moment,
                moment,
            ],
            out_specs=[
                pl.BlockSpec((total, tile), lambda i, r: (0, i)),
                pl.BlockSpec((2, 8, 3 * piece, columns), lambda i, r: (0, i, 0, 0)),
            ],
            scratch_shapes=[
                pltpu.VMEM((rows, hidden), BF),
                pltpu.VMEM((rows, 2 * hidden), BF),
                pltpu.VMEM((n, n), BF),
            ],
        ),
        out_shape=[
            jax.ShapeDtypeStruct((total, half), BF),
            jax.ShapeDtypeStruct((2, half // piece, 3 * piece, columns), BF),
        ],
        compiler_params=pltpu.CompilerParams(vmem_limit_bytes=REAR_VMEM),
        cost_estimate=pl.CostEstimate(
            flops=7 * 10**9, bytes_accessed=36 * 1024 * 1024, transcendentals=rows * hidden
        ),
        name="expert_rear",
    )(
        rank, x, c, own, other, weight.reshape(2, 2, half, columns),
        first.reshape(2, half, columns), second.reshape(2, half, columns),
    )


def combine_kernel(cap, tiles, meta_ref, back_ref, mixed_ref, grad_ref, pick):
    total = back_ref.shape[0]
    tok = mixed_ref.shape[0]
    i = pl.program_id(0)

    @pl.when(i == 0)
    def _():
        ident, part, a = row_parts((tok, total), 1, cap)
        index = ident // cap
        ident = index // 2 * cap + ident - index * cap
        chunk = (index - index // 2 * 2) * 2 + part
        hit0 = ident == meta_ref[:, 0:1].astype(jnp.int32)
        hit1 = ident == meta_ref[:, 1:2].astype(jnp.int32)
        for k in range(4):
            here = chunk == k
            out = here & (a == 0)
            pick[3 * k] = jnp.where(hit0 & out, 1.0, 0.0).astype(BF)
            pick[3 * k + 1] = jnp.where(hit1 & out, 1.0, 0.0).astype(BF)
            pick[3 * k + 2] = jnp.where((hit0 | hit1) & here & (a == 1), 1.0, 0.0).astype(BF)

    block = back_ref[...]
    for k in range(4):
        at = pl.ds(pl.multiple_of((k * tiles + i) * TILE, TILE), TILE)
        one = jnp.dot(pick[3 * k], block, preferred_element_type=F32)
        two = jnp.dot(pick[3 * k + 1], block, preferred_element_type=F32)
        both = jnp.dot(pick[3 * k + 2], block, preferred_element_type=F32)
        mixed_ref[:, at] = (one * meta_ref[:, 2:3] + two * meta_ref[:, 3:4]).astype(BF)
        grad_ref[:, at] = both.astype(BF)


def combine(meta, back, cap):
    total, half = back.shape
    tok = meta.shape[0]
    tiles = half // TILE
    whole = pl.BlockSpec((tok, 4 * half), lambda i: (0, 0))
    shape = jax.ShapeDtypeStruct((tok, 4 * half), BF)
    return pl.pallas_call(
        functools.partial(combine_kernel, cap, tiles),
        grid=(tiles,),
        in_specs=[
            pl.BlockSpec((tok, 4), lambda i: (0, 0)),
            pl.BlockSpec((total, TILE), lambda i: (0, i)),
        ],
        out_specs=[whole, whole],
        out_shape=[shape, shape],
        scratch_shapes=[pltpu.VMEM((12, tok, total), BF)],
        compiler_params=pltpu.CompilerParams(vmem_limit_bytes=COMBINE_VMEM),
        cost_estimate=pl.CostEstimate(
            flops=2 * 12 * tok * total * half, bytes_accessed=13 * MIB, transcendentals=0
        ),
        name="combine",
    )(meta, back)


def reorder_kernel(order_ref, source, out):
    def body(j, carry):
        out[j] = source[order_ref[j]]
        return carry

    lax.fori_loop(0, out.shape[0], body, 0)


def reorder(array, inverse, count):
    shape = (count, array.shape[0] // count, array.shape[1])
    whole = pl.BlockSpec(memory_space=pltpu.VMEM)
    return pl.pallas_call(
        reorder_kernel,
        in_specs=[pl.BlockSpec(memory_space=pltpu.SMEM), whole],
        out_specs=whole,
        out_shape=jax.ShapeDtypeStruct(shape, BF),
        compiler_params=pltpu.CompilerParams(vmem_limit_bytes=4 * MIB),
        cost_estimate=pl.CostEstimate(
            flops=0, bytes_accessed=4 * array.size, transcendentals=0
        ),
        name="reorder",
    )(inverse, array.reshape(shape))


def swap(array, axes="expert"):
    return lax.all_to_all(array, axes, split_axis=0, concat_axis=0, tiled=True)


def slot_table(routes, experts, cap):
    ids = routes.reshape(-1)
    labels = jnp.arange(experts, dtype=jnp.int32)
    onehot = (ids[:, None] == labels[None, :]).astype(jnp.int32)
    earlier = jnp.sum((jnp.cumsum(onehot, axis=0) - onehot) * onehot, axis=1)
    return (ids * cap + earlier).reshape(routes.shape)


def local(tokens, cotangent, gate_probs, routes, placement, weights, first_moment, second_moment):
    experts = lax.axis_size("expert")
    tok, width = tokens.shape
    top = routes.shape[1]
    cap = max(2, (3 * tok * top + 2 * experts - 1) // (2 * experts))
    labels = jnp.arange(experts, dtype=jnp.int32)
    inverse = jnp.sum(
        labels[None, :] * (placement[None, :] == labels[:, None]).astype(jnp.int32), axis=1
    )
    inverse = jnp.minimum(inverse, experts - 1)
    rank = lax.axis_index("dp")
    weight = weights[0]
    rows = weight.shape[0] // 2
    piece = rows // experts
    columns = weight.shape[1]
    both = ("expert", "dp")
    together = lax.optimization_barrier

    place = rank.reshape(1).astype(jnp.int32)
    send = dispatch(routes.T, gate_probs.T, tokens, cotangent, experts, cap)
    send, routes, probs, inverse, place = together((send, routes, gate_probs, inverse, place))
    slots = slot_table(routes, experts, cap)
    meta = jnp.concatenate([slots.astype(F32), probs], axis=1)
    send, meta = together((send, meta))
    recv = swap(send.reshape(-1, width // 4), both)
    recv, meta, inverse, place = together((recv, meta, inverse, place))
    x, c, own, out = front_call(place, recv, weight, cap)
    other = lax.ppermute(out, "dp", [(0, 1), (1, 0)])
    result, state = rear_call(
        place, x, c, own, other, weight, first_moment[0], second_moment[0], cap, piece
    )
    result, state, meta, inverse = together((result, state, meta, inverse))
    spread = swap(state.reshape(3 * rows, columns))
    spread, result, meta, inverse = together((spread, result, meta, inverse))
    ready = reorder(spread, inverse, experts).reshape(3 * rows, columns)
    ready, result, meta = together((ready, result, meta))
    back = swap(result, both)
    ready, back, meta = together((ready, back, meta))
    moved = swap(ready).reshape(experts, 3, piece, columns)
    mixed, token_grad = combine(meta, back, cap)
    m, v, step = (moved[:, k].reshape(1, rows, columns) for k in range(3))
    return (mixed, token_grad, m, v, step)


def solution(mesh):
    in_specs = (
        P(("expert", "dp"), None),
        P(("expert", "dp"), None),
        P(("expert", "dp"), None),
        P(("expert", "dp"), None),
        P(),
        P("expert", None, None),
        P("expert", "dp", None),
        P("expert", "dp", None),
    )
    out_specs = (
        P(("expert", "dp"), None),
        P(("expert", "dp"), None),
        P("expert", "dp", None),
        P("expert", "dp", None),
        P("expert", "dp", None),
    )
    return jax.shard_map(local, mesh=mesh, in_specs=in_specs, out_specs=out_specs, check_vma=False)
```

```python
import functools
import jax
import jax.numpy as jnp
from jax import lax
from jax.experimental import pallas as pl
from jax.experimental.pallas import tpu as pltpu
from jax.sharding import PartitionSpec as P

BF = jnp.bfloat16
F32 = jnp.float32
MIB = 1024 * 1024
DISPATCH_VMEM, FRONT_VMEM, SORT_VMEM = 60 * MIB, 12 * MIB, 12 * MIB
REAR_VMEM, COMBINE_VMEM = 16 * MIB, 24 * MIB
TILE = 512


def slots_of(route, experts, cap):
    tok = route.shape[1]
    label = lax.broadcasted_iota(jnp.int32, (experts, tok), 0)
    one0 = jnp.where(label == route[0:1, :], 1.0, 0.0)
    one1 = jnp.where(label == route[1:2, :], 1.0, 0.0)
    before = lax.broadcasted_iota(jnp.int32, (tok, tok), 0) < lax.broadcasted_iota(
        jnp.int32, (tok, tok), 1
    )
    count = jnp.dot(
        (one0 + one1).astype(BF),
        jnp.where(before, 1.0, 0.0).astype(BF),
        preferred_element_type=F32,
    )
    earlier0 = jnp.sum(one0 * count, axis=0, keepdims=True).astype(jnp.int32)
    earlier1 = jnp.sum(one1 * count, axis=0, keepdims=True).astype(jnp.int32)
    return route[0:1, :] * cap + earlier0, route[1:2, :] * cap + earlier1


def dispatch_kernel(
    cap, experts, route_ref, prob_ref, token_ref, cot_ref, out_ref, rows_in, low, high, scale,
    route, probs, stage, sem, out_sem
):
    tok, width = token_ref.shape
    per = 4 * cap
    small = [
        pltpu.make_async_copy(route_ref, route, sem.at[2]),
        pltpu.make_async_copy(prob_ref, probs, sem.at[3]),
    ]
    loads = [
        pltpu.make_async_copy(token_ref, rows_in.at[pl.ds(0, tok), :], sem.at[0]),
        pltpu.make_async_copy(cot_ref, rows_in.at[pl.ds(tok, tok), :], sem.at[1]),
    ]
    for load in small + loads:
        load.start()
    for load in small:
        load.wait()
    slot0, slot1 = slots_of(route[...], experts, cap)
    reach = 2 * per // 3
    shape = (experts, reach, tok)
    for half, ref in ((0, low), (1, high)):
        at = lax.broadcasted_iota(jnp.int32, shape, 1) + half * (reach // 2 - 2 * cap)
        ok = (at >= 0) & (at < 2 * cap)
        a = jnp.where(at >= cap, 1, 0)
        ident = lax.broadcasted_iota(jnp.int32, shape, 0) * cap + at - cap * a
        ident = jnp.where(ok, ident, -1).reshape(experts * reach, tok)
        a = a.reshape(experts * reach, tok)
        hit0 = ident == slot0
        hit1 = ident == slot1
        hit = hit0 | hit1
        for kind in (0, 1):
            ref[:, kind * tok : (kind + 1) * tok] = jnp.where(
                hit & (a == kind), 1.0, 0.0
            ).astype(BF)
        prob = jnp.where(hit0, probs[0:1, :], 0.0) + jnp.where(hit1, probs[1:2, :], 0.0)
        prob = jnp.sum(prob, axis=1, keepdims=True)
        scale[half] = jnp.where(a == 0, 1.0, prob)
    for load in loads:
        load.wait()
    half_width = width // 4
    lot = 16

    tiles = half_width // TILE
    sends = [
        pltpu.make_async_copy(
            stage.at[i], out_ref.at[:, :, :, pl.ds(i * TILE, TILE)], out_sem.at[i]
        )
        for i in range(tiles)
    ]
    for i in range(tiles):
        for r in range(2):
            first, second = (
                rows_in[:, (2 * r + h) * half_width + i * TILE :][:, :TILE] for h in range(2)
            )

            def body(g, carry):
                part = pl.ds(pl.multiple_of(g * lot * reach, lot * reach), lot * reach)
                y0 = jnp.dot(low[part, :], first, preferred_element_type=F32)
                y1 = jnp.dot(high[part, :], second, preferred_element_type=F32)
                y0 = y0 * scale[0, part, 0:1]
                y1 = y1 * scale[1, part, 0:1]
                mid = reach // 2
                for j in range(lot):
                    base = j * reach
                    made = [
                        y0[base : base + mid],
                        y0[base + mid : base + reach] + y1[base : base + mid],
                        y1[base + mid : base + reach],
                    ]
                    stage[i, g * lot + j, r] = jnp.concatenate(made, axis=0).astype(BF)
                return carry

            lax.fori_loop(0, experts // lot, body, 0)
        sends[i].start()
    for send in sends:
        send.wait()


def dispatch(routes, probs, tokens, cotangent, experts, cap):
    tok, width = tokens.shape
    half = width // 4
    per = 4 * cap
    rows = experts * per * 2 // 3
    anywhere = pl.BlockSpec(memory_space=pltpu.HBM)
    return pl.pallas_call(
        functools.partial(dispatch_kernel, cap, experts),
        in_specs=[anywhere] * 4,
        out_specs=anywhere,
        out_shape=jax.ShapeDtypeStruct((experts, 2, per, half), BF),
        scratch_shapes=[
            pltpu.VMEM((2 * tok, width), BF),
            pltpu.VMEM((rows, 2 * tok), BF),
            pltpu.VMEM((rows, 2 * tok), BF),
            pltpu.VMEM((2, rows, 128), F32),
            pltpu.VMEM((2, tok), jnp.int32),
            pltpu.VMEM((2, tok), F32),
            pltpu.VMEM((half // TILE, experts, 2, per, TILE), BF),
            pltpu.SemaphoreType.DMA((4,)),
            pltpu.SemaphoreType.DMA((half // TILE,)),
        ],
        compiler_params=pltpu.CompilerParams(vmem_limit_bytes=DISPATCH_VMEM),
        cost_estimate=pl.CostEstimate(
            flops=3 * 10**9, bytes_accessed=13 * MIB, transcendentals=0
        ),
        name="dispatch",
    )(routes, probs, tokens, cotangent)


def order_matrix(group, cap, inverse):
    n = group * cap * 4
    i = lax.broadcasted_iota(jnp.int32, (n, n), 1 if inverse else 0)
    j = lax.broadcasted_iota(jnp.int32, (n, n), 0 if inverse else 1)
    hk = i // (group * cap)
    rest = i - hk * (group * cap)
    src = rest // cap
    slot = rest - src * cap
    return jnp.where(src * (4 * cap) + hk * cap + slot == j, 1.0, 0.0).astype(BF)


def unmix(fore, recv_ref, first, columns, group, cap):
    n = group * cap
    span = 4 * n
    made = [[] for _ in range(4)]
    for g in range(first.stop // span - first.start // span):
        rows = slice(first.start + g * span, first.start + (g + 1) * span)
        got = jnp.dot(
            fore, recv_ref[rows, columns], preferred_element_type=F32
        ).astype(BF)
        for k in range(4):
            made[k].append(got[k * n : (k + 1) * n])
    return made


def front_kernel(cap, group, part, rank_ref, recv_ref, w_ref, sum_ref, send_ref):
    total = recv_ref.shape[0] // 2
    columns = sum_ref.shape[1]
    front = columns // 3 * 2
    rank = rank_ref[0]
    fore = order_matrix(group, cap, False)
    sum_ref[...] = jnp.zeros_like(sum_ref)

    def body(i, carry):
        at = pl.ds(pl.multiple_of(i * TILE, TILE), TILE)
        made = unmix(fore, recv_ref, slice(part * total, (part + 1) * total), at, group, cap)
        for h in range(2):
            x = jnp.concatenate(made[2 * h], axis=0)
            c = jnp.concatenate(made[2 * h + 1], axis=0)
            w = w_ref[rank, h, at, :]
            sum_ref[:, :front] += jnp.dot(x, w[:, :front], preferred_element_type=F32)
            sum_ref[:, front:] += jnp.dot(c, w[:, front:], preferred_element_type=F32)
        return carry

    lax.fori_loop(0, recv_ref.shape[1] // TILE, body, 0)
    send_ref[...] = sum_ref[...].astype(BF)


def sort_kernel(cap, group, recv_ref, x_ref, c_ref):
    n = group * cap
    fore = order_matrix(group, cap, False)

    def body(i, carry):
        at = pl.ds(pl.multiple_of(i * TILE, TILE), TILE)
        made = unmix(fore, recv_ref, slice(0, recv_ref.shape[0]), at, group, cap)
        for g in range(len(made[0])):
            rows = slice(g * n, (g + 1) * n)
            for h in range(2):
                x_ref[h, rows, at] = made[2 * h][g]
                c_ref[h, rows, at] = made[2 * h + 1][g]
        return carry

    lax.fori_loop(0, recv_ref.shape[1] // TILE, body, 0)


GROUP = 8
PIECES = 8


def held():
    return pl.BlockSpec(memory_space=pltpu.VMEM)


def scalars():
    return pl.BlockSpec(memory_space=pltpu.SMEM)


def front_call(rank, recv, weight, cap, part):
    total, half = recv.shape
    columns = weight.shape[-1]
    rows = total // 8
    return pl.pallas_call(
        functools.partial(front_kernel, cap, GROUP, part),
        in_specs=[scalars(), held(), held()],
        out_specs=[held(), held()],
        out_shape=[
            jax.ShapeDtypeStruct((rows, columns), F32),
            jax.ShapeDtypeStruct((rows, columns), BF),
        ],
        compiler_params=pltpu.CompilerParams(vmem_limit_bytes=FRONT_VMEM),
        cost_estimate=pl.CostEstimate(
            flops=2 * 10**9, bytes_accessed=7 * MIB, transcendentals=0
        ),
        name="expert_front",
    )(rank, recv, weight)


def sort_call(recv, cap):
    total, half = recv.shape
    rows = total // 4
    return pl.pallas_call(
        functools.partial(sort_kernel, cap, GROUP),
        in_specs=[held()],
        out_specs=[held(), held()],
        out_shape=[jax.ShapeDtypeStruct((2, rows, half), BF)] * 2,
        compiler_params=pltpu.CompilerParams(vmem_limit_bytes=SORT_VMEM),
        cost_estimate=pl.CostEstimate(
            flops=2 * 10**9, bytes_accessed=19 * MIB, transcendentals=0
        ),
        name="sort_rows",
    )(recv)


def rear_kernel(
    cap, group, piece, rank_ref, x_ref, c_ref, own0, own1, other0, other1, w_ref, first_ref,
    second_ref, out_ref, state_ref, inner, pre
):
    n = group * cap
    span = 4 * n
    sets = out_ref.shape[0] // span
    hidden = inner.shape[1]
    tile = PIECES * piece
    rank = rank_ref[0]
    back = order_matrix(group, cap, True)
    total = jnp.concatenate(
        [own0[...] + other0[...].astype(F32), own1[...] + other1[...].astype(F32)], axis=0
    )
    gate = total[:, :hidden]
    up = total[:, hidden : 2 * hidden]
    grad = total[:, 2 * hidden :]
    sig = jax.nn.sigmoid(gate)
    active = gate * sig
    inner[...] = (active * up).astype(BF)
    slope = sig * (1.0 + gate * (1.0 - sig))
    pre[:, :hidden] = (grad * up * slope).astype(BF)
    pre[:, hidden:] = (grad * active).astype(BF)
    contract = (((1,), (1,)), ((), ()))
    lead = (((0,), (0,)), ((), ()))

    def body(i, carry):
        cols = pl.ds(pl.multiple_of(i * tile, tile), tile)
        made = []
        for h in range(2):
            for factor, at in (
                (inner, slice(2 * hidden, 3 * hidden)),
                (pre, slice(0, 2 * hidden)),
            ):
                made.append(
                    lax.dot_general(
                        factor[...], w_ref[rank, h, cols, at], contract,
                        preferred_element_type=F32,
                    ).astype(BF)
                )
        for g in range(sets):
            stack = jnp.concatenate([m[g * n : (g + 1) * n] for m in made], axis=0)
            out_ref[g * span : (g + 1) * span, cols] = jnp.dot(
                back, stack, preferred_element_type=F32
            ).astype(BF)
        for h in range(2):
            for source, factor, at in (
                (x_ref, pre, slice(0, 2 * hidden)),
                (c_ref, inner, slice(2 * hidden, 3 * hidden)),
            ):
                grad = lax.dot_general(
                    source[h, :, cols], factor[...], lead, preferred_element_type=F32
                )
                m = 0.9 * first_ref[h, cols, at].astype(F32) + 0.1 * grad
                v = 0.95 * second_ref[h, cols, at].astype(F32) + 0.05 * grad * grad
                step = m / (jnp.sqrt(v) + 1e-08) + 0.1 * w_ref[rank, h, cols, at].astype(F32)
                for k, value in enumerate((m, v, step)):
                    value = value.astype(BF)
                    for j in range(PIECES):
                        state_ref[h, i * PIECES + j, k * piece : (k + 1) * piece, at] = value[
                            j * piece : (j + 1) * piece
                        ]
        return carry

    lax.fori_loop(0, out_ref.shape[1] // tile, body, 0)


def rear_call(rank, x, c, own, other, weight, first, second, cap, piece):
    rows, half = x.shape[1:]
    columns = weight.shape[-1]
    hidden = columns // 3
    total = 4 * rows
    return pl.pallas_call(
        functools.partial(rear_kernel, cap, GROUP, piece),
        in_specs=[scalars()] + [held()] * 9,
        out_specs=[held(), held()],
        scratch_shapes=[pltpu.VMEM((rows, hidden), BF), pltpu.VMEM((rows, 2 * hidden), BF)],
        out_shape=[
            jax.ShapeDtypeStruct((total, half), BF),
            jax.ShapeDtypeStruct((2, half // piece, 3 * piece, columns), BF),
        ],
        compiler_params=pltpu.CompilerParams(vmem_limit_bytes=REAR_VMEM),
        cost_estimate=pl.CostEstimate(
            flops=7 * 10**9, bytes_accessed=36 * MIB, transcendentals=rows * hidden
        ),
        name="expert_rear",
    )(
        rank, x, c, *own, *other, weight,
        first.reshape(2, half, columns), second.reshape(2, half, columns),
    )


def column(row):
    n = row.shape[1]
    same = lax.broadcasted_iota(jnp.int32, (n, n), 0) == lax.broadcasted_iota(
        jnp.int32, (n, n), 1
    )
    return jnp.sum(jnp.where(same, row, jnp.zeros_like(row)), axis=1, keepdims=True)


def combine_kernel(
    cap, group, experts, route_ref, prob_ref, back_ref, mixed_ref, grad_ref, stage, pick, both
):
    total, half = back_ref.shape
    tok = mixed_ref.shape[0]
    n = group * cap
    rows = total // 4
    fore = order_matrix(group, cap, False)
    slot0, slot1 = slots_of(route_ref[...], experts, cap)
    prob0, prob1 = column(prob_ref[0:1, :]), column(prob_ref[1:2, :])
    r = lax.broadcasted_iota(jnp.int32, (tok, rows), 1)
    source = r // cap
    expert = source // 2
    ident = expert * cap + r - source * cap
    part = source - 2 * expert
    hit0 = ident == column(slot0)
    hit1 = ident == column(slot1)
    for k in range(2):
        here = part == k
        at = 2 * k * tok
        pick[at : at + tok, :] = jnp.where(hit0 & here, 1.0, 0.0).astype(BF)
        pick[at + tok : at + 2 * tok, :] = jnp.where(hit1 & here, 1.0, 0.0).astype(BF)
        both[k * tok : (k + 1) * tok, :] = jnp.where((hit0 | hit1) & here, 1.0, 0.0).astype(BF)

    def body(i, carry):
        at = pl.ds(pl.multiple_of(i * TILE, TILE), TILE)
        made = unmix(fore, back_ref, slice(0, total), at, group, cap)
        for k in range(4):
            for g in range(len(made[k])):
                stage[k, g * n : (g + 1) * n, :] = made[k][g]
        for h in range(2):
            out = jnp.dot(pick[...], stage[2 * h], preferred_element_type=F32)
            grad = jnp.dot(both[...], stage[2 * h + 1], preferred_element_type=F32)
            for k in range(2):
                to = pl.ds(pl.multiple_of((2 * k + h) * half + i * TILE, TILE), TILE)
                one = out[2 * k * tok : (2 * k + 1) * tok]
                two = out[(2 * k + 1) * tok : (2 * k + 2) * tok]
                mixed_ref[:, to] = (one * prob0 + two * prob1).astype(BF)
                grad_ref[:, to] = grad[k * tok : (k + 1) * tok].astype(BF)
        return carry

    lax.fori_loop(0, half // TILE, body, 0)


def combine(routes, probs, back, experts, cap):
    total, half = back.shape
    tok = routes.shape[1]
    shape = jax.ShapeDtypeStruct((tok, 4 * half), BF)
    return pl.pallas_call(
        functools.partial(combine_kernel, cap, GROUP, experts),
        in_specs=[held()] * 3,
        out_specs=[held(), held()],
        out_shape=[shape, shape],
        scratch_shapes=[
            pltpu.VMEM((4, total // 4, TILE), BF),
            pltpu.VMEM((4 * tok, total // 4), BF),
            pltpu.VMEM((2 * tok, total // 4), BF),
        ],
        compiler_params=pltpu.CompilerParams(vmem_limit_bytes=COMBINE_VMEM),
        cost_estimate=pl.CostEstimate(
            flops=6 * 10**9, bytes_accessed=13 * MIB, transcendentals=0
        ),
        name="combine",
    )(routes, probs, back)


def reorder_kernel(order_ref, source, out):
    def body(j, carry):
        out[j] = source[order_ref[j]]
        return carry

    lax.fori_loop(0, out.shape[0], body, 0)


def reorder(array, inverse, count):
    shape = (count, array.shape[0] // count, array.shape[1])
    whole = pl.BlockSpec(memory_space=pltpu.VMEM)
    return pl.pallas_call(
        reorder_kernel,
        in_specs=[pl.BlockSpec(memory_space=pltpu.SMEM), whole],
        out_specs=whole,
        out_shape=jax.ShapeDtypeStruct(shape, BF),
        compiler_params=pltpu.CompilerParams(vmem_limit_bytes=4 * MIB),
        cost_estimate=pl.CostEstimate(
            flops=0, bytes_accessed=4 * array.size, transcendentals=0
        ),
        name="reorder",
    )(inverse, array.reshape(shape))


def swap(array, axes="expert"):
    return lax.all_to_all(array, axes, split_axis=0, concat_axis=0, tiled=True)


def split_kernel(source, *refs):
    outs, sem = refs[:3], refs[3]
    piece = outs[0].shape[1]
    copies = [
        pltpu.make_async_copy(source.at[:, pl.ds(k * piece, piece), :], out, sem.at[k])
        for k, out in enumerate(outs)
    ]
    for copy in copies:
        copy.start()
    for copy in copies:
        copy.wait()


def split(moved):
    count, rows, columns = moved.shape
    return pl.pallas_call(
        split_kernel,
        in_specs=[held()],
        out_specs=[pl.BlockSpec(memory_space=pl.ANY)] * 3,
        out_shape=[jax.ShapeDtypeStruct((count, rows // 3, columns), BF)] * 3,
        scratch_shapes=[pltpu.SemaphoreType.DMA((3,))],
        compiler_params=pltpu.CompilerParams(vmem_limit_bytes=4 * MIB),
        cost_estimate=pl.CostEstimate(flops=0, bytes_accessed=4 * moved.size, transcendentals=0),
        name="split",
    )(moved)


def local(tokens, cotangent, gate_probs, routes, placement, weights, first_moment, second_moment):
    experts = lax.axis_size("expert")
    tok, width = tokens.shape
    top = routes.shape[1]
    cap = max(2, (3 * tok * top + 2 * experts - 1) // (2 * experts))
    rank = lax.axis_index("dp")
    weight = weights[0]
    rows = weight.shape[0] // 2
    piece = rows // experts
    columns = weight.shape[1]
    both = ("expert", "dp")
    together = lax.optimization_barrier

    place = rank.reshape(1).astype(jnp.int32)
    labels = jnp.arange(experts, dtype=jnp.int32)
    inverse = jnp.sum(
        labels[None, :] * (placement[None, :] == labels[:, None]).astype(jnp.int32), axis=1
    )
    inverse = jnp.minimum(inverse, experts - 1)
    send = dispatch(routes.T, gate_probs.T, tokens, cotangent, experts, cap)
    send, inverse, place = together((send, inverse, place))
    recv = swap(send.reshape(-1, width // 4), both)
    weight = weight.reshape(2, 2, rows // 2, columns)
    recv, inverse, place = together((recv, inverse, place))
    own0, out0 = front_call(place, recv, weight, cap, 0)
    own1, out1 = front_call(place, recv, weight, cap, 1)
    other = [lax.ppermute(out, "dp", [(0, 1), (1, 0)]) for out in (out0, out1)]
    recv, own1 = together((recv, own1))
    x, c = sort_call(recv, cap)
    result, state = rear_call(
        place, x, c, [own0, own1], other, weight, first_moment[0], second_moment[0], cap, piece
    )
    result, state, inverse = together((result, state, inverse))
    spread = swap(state.reshape(3 * rows, columns))
    spread, result, inverse = together((spread, result, inverse))
    ready = reorder(spread, inverse, experts).reshape(3 * rows, columns)
    ready, result = together((ready, result))
    back = swap(result, both)
    mixed, token_grad = combine(routes.T, gate_probs.T, back, experts, cap)
    ready, mixed, token_grad = together((ready, mixed, token_grad))
    moved = swap(ready).reshape(experts, 3 * piece, columns)
    m, v, step = (array.reshape(1, rows, columns) for array in split(moved))
    return (mixed, token_grad, m, v, step)


def solution(mesh):
    in_specs = (
        P(("expert", "dp"), None),
        P(("expert", "dp"), None),
        P(("expert", "dp"), None),
        P(("expert", "dp"), None),
        P(),
        P("expert", None, None),
        P("expert", "dp", None),
        P("expert", "dp", None),
    )
    out_specs = (
        P(("expert", "dp"), None),
        P(("expert", "dp"), None),
        P("expert", "dp", None),
        P("expert", "dp", None),
        P("expert", "dp", None),
    )
    return jax.shard_map(local, mesh=mesh, in_specs=in_specs, out_specs=out_specs, check_vma=False)
```

```python
import functools
import jax
import jax.numpy as jnp
from jax import lax
from jax.experimental import pallas as pl
from jax.experimental.pallas import tpu as pltpu
from jax.sharding import PartitionSpec as P

BF = jnp.bfloat16
F32 = jnp.float32
MIB = 1024 * 1024
DISPATCH_VMEM, FRONT_VMEM, SORT_VMEM = 60 * MIB, 12 * MIB, 12 * MIB
REAR_VMEM, COMBINE_VMEM = 12 * MIB, 16 * MIB
TILE = 512


def slots_of(route, experts, cap):
    tok = route.shape[1]
    label = lax.broadcasted_iota(jnp.int32, (experts, tok), 0)
    one0 = jnp.where(label == route[0:1, :], 1.0, 0.0)
    one1 = jnp.where(label == route[1:2, :], 1.0, 0.0)
    before = lax.broadcasted_iota(jnp.int32, (tok, tok), 0) < lax.broadcasted_iota(
        jnp.int32, (tok, tok), 1
    )
    count = jnp.dot(
        (one0 + one1).astype(BF),
        jnp.where(before, 1.0, 0.0).astype(BF),
        preferred_element_type=F32,
    )
    earlier0 = jnp.sum(one0 * count, axis=0, keepdims=True).astype(jnp.int32)
    earlier1 = jnp.sum(one1 * count, axis=0, keepdims=True).astype(jnp.int32)
    return route[0:1, :] * cap + earlier0, route[1:2, :] * cap + earlier1


def dispatch_kernel(
    cap, experts, route_ref, prob_ref, token_ref, cot_ref, out_ref, rows_in, low, high, scale,
    route, probs, stage, sem, out_sem
):
    tok, width = token_ref.shape
    per = 4 * cap
    small = [
        pltpu.make_async_copy(route_ref, route, sem.at[2]),
        pltpu.make_async_copy(prob_ref, probs, sem.at[3]),
    ]
    loads = [
        pltpu.make_async_copy(token_ref, rows_in.at[pl.ds(0, tok), :], sem.at[0]),
        pltpu.make_async_copy(cot_ref, rows_in.at[pl.ds(tok, tok), :], sem.at[1]),
    ]
    for load in small + loads:
        load.start()
    for load in small:
        load.wait()
    slot0, slot1 = slots_of(route[...], experts, cap)
    reach = 2 * per // 3
    shape = (experts, reach, tok)
    for half, ref in ((0, low), (1, high)):
        at = lax.broadcasted_iota(jnp.int32, shape, 1) + half * (reach // 2 - 2 * cap)
        ok = (at >= 0) & (at < 2 * cap)
        a = jnp.where(at >= cap, 1, 0)
        ident = lax.broadcasted_iota(jnp.int32, shape, 0) * cap + at - cap * a
        ident = jnp.where(ok, ident, -1).reshape(experts * reach, tok)
        a = a.reshape(experts * reach, tok)
        hit0 = ident == slot0
        hit1 = ident == slot1
        hit = hit0 | hit1
        for kind in (0, 1):
            ref[:, kind * tok : (kind + 1) * tok] = jnp.where(
                hit & (a == kind), 1.0, 0.0
            ).astype(BF)
        prob = jnp.where(hit0, probs[0:1, :], 0.0) + jnp.where(hit1, probs[1:2, :], 0.0)
        prob = jnp.sum(prob, axis=1, keepdims=True)
        scale[half] = jnp.where(a == 0, 1.0, prob)
    for load in loads:
        load.wait()
    half_width = width // 4
    lot = 16

    tiles = half_width // TILE
    sends = [
        pltpu.make_async_copy(
            stage.at[i], out_ref.at[:, :, :, pl.ds(i * TILE, TILE)], out_sem.at[i]
        )
        for i in range(tiles)
    ]
    for i in range(tiles):
        for r in range(2):
            first, second = (
                rows_in[:, (2 * r + h) * half_width + i * TILE :][:, :TILE] for h in range(2)
            )

            def body(g, carry):
                part = pl.ds(pl.multiple_of(g * lot * reach, lot * reach), lot * reach)
                y0 = jnp.dot(low[part, :], first, preferred_element_type=F32)
                y1 = jnp.dot(high[part, :], second, preferred_element_type=F32)
                y0 = y0 * scale[0, part, 0:1]
                y1 = y1 * scale[1, part, 0:1]
                mid = reach // 2
                for j in range(lot):
                    base = j * reach
                    made = [
                        y0[base : base + mid],
                        y0[base + mid : base + reach] + y1[base : base + mid],
                        y1[base + mid : base + reach],
                    ]
                    stage[i, g * lot + j, r] = jnp.concatenate(made, axis=0).astype(BF)
                return carry

            lax.fori_loop(0, experts // lot, body, 0)
        sends[i].start()
    for send in sends:
        send.wait()


def dispatch(routes, probs, tokens, cotangent, experts, cap):
    tok, width = tokens.shape
    half = width // 4
    per = 4 * cap
    rows = experts * per * 2 // 3
    anywhere = pl.BlockSpec(memory_space=pltpu.HBM)
    return pl.pallas_call(
        functools.partial(dispatch_kernel, cap, experts),
        in_specs=[anywhere] * 4,
        out_specs=anywhere,
        out_shape=jax.ShapeDtypeStruct((experts, 2, per, half), BF),
        scratch_shapes=[
            pltpu.VMEM((2 * tok, width), BF),
            pltpu.VMEM((rows, 2 * tok), BF),
            pltpu.VMEM((rows, 2 * tok), BF),
            pltpu.VMEM((2, rows, 128), F32),
            pltpu.VMEM((2, tok), jnp.int32),
            pltpu.VMEM((2, tok), F32),
            pltpu.VMEM((half // TILE, experts, 2, per, TILE), BF),
            pltpu.SemaphoreType.DMA((4,)),
            pltpu.SemaphoreType.DMA((half // TILE,)),
        ],
        compiler_params=pltpu.CompilerParams(vmem_limit_bytes=DISPATCH_VMEM),
        cost_estimate=pl.CostEstimate(
            flops=3 * 10**9, bytes_accessed=13 * MIB, transcendentals=0
        ),
        name="dispatch",
    )(routes, probs, tokens, cotangent)


def order_matrix(group, cap, inverse):
    n = group * cap * 4
    i = lax.broadcasted_iota(jnp.int32, (n, n), 1 if inverse else 0)
    j = lax.broadcasted_iota(jnp.int32, (n, n), 0 if inverse else 1)
    hk = i // (group * cap)
    rest = i - hk * (group * cap)
    src = rest // cap
    slot = rest - src * cap
    return jnp.where(src * (4 * cap) + hk * cap + slot == j, 1.0, 0.0).astype(BF)


def unmix(fore, recv_ref, first, columns, group, cap):
    n = group * cap
    span = 4 * n
    made = [[] for _ in range(4)]
    for g in range(first.stop // span - first.start // span):
        rows = slice(first.start + g * span, first.start + (g + 1) * span)
        got = jnp.dot(
            fore, recv_ref[rows, columns], preferred_element_type=F32
        ).astype(BF)
        for k in range(4):
            made[k].append(got[k * n : (k + 1) * n])
    return made


def front_kernel(cap, group, part, rank_ref, recv_ref, w_ref, sum_ref, send_ref):
    total = recv_ref.shape[0] // 2
    columns = sum_ref.shape[1]
    front = columns // 3 * 2
    rank = rank_ref[0]
    fore = order_matrix(group, cap, False)
    sum_ref[...] = jnp.zeros_like(sum_ref)

    def body(i, carry):
        at = pl.ds(pl.multiple_of(i * TILE, TILE), TILE)
        made = unmix(fore, recv_ref, slice(part * total, (part + 1) * total), at, group, cap)
        for h in range(2):
            x = jnp.concatenate(made[2 * h], axis=0)
            c = jnp.concatenate(made[2 * h + 1], axis=0)
            w = w_ref[rank, h, at, :]
            sum_ref[:, :front] += jnp.dot(x, w[:, :front], preferred_element_type=F32)
            sum_ref[:, front:] += jnp.dot(c, w[:, front:], preferred_element_type=F32)
        return carry

    lax.fori_loop(0, recv_ref.shape[1] // TILE, body, 0)
    send_ref[...] = sum_ref[...].astype(BF)


def sort_kernel(cap, group, recv_ref, x_ref, c_ref):
    n = group * cap
    fore = order_matrix(group, cap, False)

    def body(i, carry):
        at = pl.ds(pl.multiple_of(i * TILE, TILE), TILE)
        made = unmix(fore, recv_ref, slice(0, recv_ref.shape[0]), at, group, cap)
        for g in range(len(made[0])):
            rows = slice(g * n, (g + 1) * n)
            for h in range(2):
                x_ref[h, rows, at] = made[2 * h][g]
                c_ref[h, rows, at] = made[2 * h + 1][g]
        return carry

    lax.fori_loop(0, recv_ref.shape[1] // TILE, body, 0)


GROUP = 8


def held():
    return pl.BlockSpec(memory_space=pltpu.VMEM)


def scalars():
    return pl.BlockSpec(memory_space=pltpu.SMEM)


def front_call(rank, recv, weight, cap, part):
    total, half = recv.shape
    columns = weight.shape[-1]
    rows = total // 8
    return pl.pallas_call(
        functools.partial(front_kernel, cap, GROUP, part),
        in_specs=[scalars(), held(), held()],
        out_specs=[held(), held()],
        out_shape=[
            jax.ShapeDtypeStruct((rows, columns), F32),
            jax.ShapeDtypeStruct((rows, columns), BF),
        ],
        compiler_params=pltpu.CompilerParams(vmem_limit_bytes=FRONT_VMEM),
        cost_estimate=pl.CostEstimate(
            flops=2 * 10**9, bytes_accessed=7 * MIB, transcendentals=0
        ),
        name="expert_front",
    )(rank, recv, weight)


def sort_call(recv, cap):
    total, half = recv.shape
    rows = total // 4
    return pl.pallas_call(
        functools.partial(sort_kernel, cap, GROUP),
        in_specs=[held()],
        out_specs=[held(), held()],
        out_shape=[jax.ShapeDtypeStruct((2, rows, half), BF)] * 2,
        compiler_params=pltpu.CompilerParams(vmem_limit_bytes=SORT_VMEM),
        cost_estimate=pl.CostEstimate(
            flops=2 * 10**9, bytes_accessed=19 * MIB, transcendentals=0
        ),
        name="sort_rows",
    )(recv)


def rear_kernel(
    cap, group, piece, rank_ref, x_ref, c_ref, own0, own1, other0, other1, w_ref, first_ref,
    second_ref, out_ref, inner, pre
):
    n = group * cap
    per = 4 * cap
    sets = out_ref.shape[0] // group
    tiles, tile = out_ref.shape[1] - 3, out_ref.shape[3]
    hidden = inner.shape[1]
    rank = rank_ref[0]
    back = order_matrix(group, cap, True)
    total = jnp.concatenate(
        [own0[...] + other0[...].astype(F32), own1[...] + other1[...].astype(F32)], axis=0
    )
    gate = total[:, :hidden]
    up = total[:, hidden : 2 * hidden]
    grad = total[:, 2 * hidden :]
    sig = jax.nn.sigmoid(gate)
    active = gate * sig
    inner[...] = (active * up).astype(BF)
    slope = sig * (1.0 + gate * (1.0 - sig))
    pre[:, :hidden] = (grad * up * slope).astype(BF)
    pre[:, hidden:] = (grad * active).astype(BF)
    contract = (((1,), (1,)), ((), ()))
    lead = (((0,), (0,)), ((), ()))

    def body(i, carry):
        cols = pl.ds(pl.multiple_of(i * tile, tile), tile)
        made = []
        for h in range(2):
            for factor, at in (
                (inner, slice(2 * hidden, 3 * hidden)),
                (pre, slice(0, 2 * hidden)),
            ):
                made.append(
                    lax.dot_general(
                        factor[...], w_ref[rank, h, cols, at], contract,
                        preferred_element_type=F32,
                    ).astype(BF)
                )
        for g in range(sets):
            stack = jnp.concatenate([m[g * n : (g + 1) * n] for m in made], axis=0)
            mixed = jnp.dot(back, stack, preferred_element_type=F32)
            for j in range(group):
                out_ref[g * group + j, i] = mixed[j * per : (j + 1) * per].astype(BF)
        for h in range(2):
            for source, factor, at in (
                (x_ref, pre, slice(0, 2 * hidden)),
                (c_ref, inner, slice(2 * hidden, 3 * hidden)),
            ):
                grad = lax.dot_general(
                    source[h, :, cols], factor[...], lead, preferred_element_type=F32
                )
                m = 0.9 * first_ref[h, cols, at].astype(F32) + 0.1 * grad
                v = 0.95 * second_ref[h, cols, at].astype(F32) + 0.05 * grad * grad
                step = m / (jnp.sqrt(v) + 1e-08) + 0.1 * w_ref[rank, h, cols, at].astype(F32)
                count = tile // piece
                for k, value in enumerate((m, v, step)):
                    for j in range(count):
                        out_ref[(h * tiles + i) * count + j, tiles + k, :, at] = value[
                            j * piece : (j + 1) * piece
                        ].astype(BF)
        return carry

    lax.fori_loop(0, tiles, body, 0)


def rear_call(rank, x, c, own, other, weight, first, second, cap, piece):
    rows, half = x.shape[1:]
    columns = weight.shape[-1]
    hidden = columns // 3
    tile = 3 * hidden
    tiles = half // tile
    return pl.pallas_call(
        functools.partial(rear_kernel, cap, GROUP, piece),
        in_specs=[scalars()] + [held()] * 9,
        out_specs=held(),
        scratch_shapes=[pltpu.VMEM((rows, hidden), BF), pltpu.VMEM((rows, 2 * hidden), BF)],
        out_shape=jax.ShapeDtypeStruct((rows // cap, tiles + 3, piece, tile), BF),
        compiler_params=pltpu.CompilerParams(vmem_limit_bytes=REAR_VMEM),
        cost_estimate=pl.CostEstimate(
            flops=7 * 10**9, bytes_accessed=36 * MIB, transcendentals=rows * hidden
        ),
        name="expert_rear",
    )(
        rank, x, c, *own, *other, weight,
        first.reshape(2, half, columns), second.reshape(2, half, columns),
    )


def column(row):
    n = row.shape[1]
    same = lax.broadcasted_iota(jnp.int32, (n, n), 0) == lax.broadcasted_iota(
        jnp.int32, (n, n), 1
    )
    return jnp.sum(jnp.where(same, row, jnp.zeros_like(row)), axis=1, keepdims=True)


def combine_kernel(
    cap, group, experts, route_ref, prob_ref, back_ref, mixed_ref, grad_ref, stage, pick, both
):
    sources, _, per, tile = back_ref.shape
    tok, width = mixed_ref.shape
    half = width // 4
    n = group * cap
    rows = sources * cap
    fore = order_matrix(group, cap, False)
    slot0, slot1 = slots_of(route_ref[...], experts, cap)
    prob0, prob1 = column(prob_ref[0:1, :]), column(prob_ref[1:2, :])
    r = lax.broadcasted_iota(jnp.int32, (tok, rows), 1)
    source = r // cap
    expert = source // 2
    ident = expert * cap + r - source * cap
    part = source - 2 * expert
    hit0 = ident == column(slot0)
    hit1 = ident == column(slot1)
    for k in range(2):
        here = part == k
        at = 2 * k * tok
        pick[at : at + tok, :] = jnp.where(hit0 & here, 1.0, 0.0).astype(BF)
        pick[at + tok : at + 2 * tok, :] = jnp.where(hit1 & here, 1.0, 0.0).astype(BF)
        both[k * tok : (k + 1) * tok, :] = jnp.where((hit0 | hit1) & here, 1.0, 0.0).astype(BF)

    def body(i, carry):
        for g in range(sources // group):
            block = back_ref[g * group : (g + 1) * group, i].reshape(group * per, tile)
            got = jnp.dot(fore, block, preferred_element_type=F32).astype(BF)
            for k in range(4):
                stage[k, g * n : (g + 1) * n, :] = got[k * n : (k + 1) * n]
        for h in range(2):
            out = jnp.dot(pick[...], stage[2 * h], preferred_element_type=F32)
            grad = jnp.dot(both[...], stage[2 * h + 1], preferred_element_type=F32)
            for k in range(2):
                to = pl.ds(pl.multiple_of((2 * k + h) * half + i * tile, tile), tile)
                one = out[2 * k * tok : (2 * k + 1) * tok]
                two = out[(2 * k + 1) * tok : (2 * k + 2) * tok]
                mixed_ref[:, to] = (one * prob0 + two * prob1).astype(BF)
                grad_ref[:, to] = grad[k * tok : (k + 1) * tok].astype(BF)
        return carry

    lax.fori_loop(0, half // tile, body, 0)


def combine(routes, probs, back, experts, cap):
    sources, slabs, _, tile = back.shape
    rows = sources * cap
    tok = routes.shape[1]
    shape = jax.ShapeDtypeStruct((tok, 4 * (slabs - 3) * tile), BF)
    return pl.pallas_call(
        functools.partial(combine_kernel, cap, GROUP, experts),
        in_specs=[held()] * 3,
        out_specs=[held(), held()],
        out_shape=[shape, shape],
        scratch_shapes=[
            pltpu.VMEM((4, rows, tile), BF),
            pltpu.VMEM((4 * tok, rows), BF),
            pltpu.VMEM((2 * tok, rows), BF),
        ],
        compiler_params=pltpu.CompilerParams(vmem_limit_bytes=COMBINE_VMEM),
        cost_estimate=pl.CostEstimate(
            flops=6 * 10**9, bytes_accessed=13 * MIB, transcendentals=0
        ),
        name="combine",
    )(routes, probs, back)


def reorder_kernel(order_ref, source, out):
    def body(j, carry):
        for r in range(2):
            out[2 * j + r] = source[2 * order_ref[j] + r, -3:]
        return carry

    lax.fori_loop(0, out.shape[0] // 2, body, 0)


def reorder(array, inverse):
    sources, _, piece, columns = array.shape
    return pl.pallas_call(
        reorder_kernel,
        in_specs=[scalars(), held()],
        out_specs=held(),
        out_shape=jax.ShapeDtypeStruct((sources, 3, piece, columns), BF),
        compiler_params=pltpu.CompilerParams(vmem_limit_bytes=4 * MIB),
        cost_estimate=pl.CostEstimate(
            flops=0, bytes_accessed=12 * sources * piece * columns, transcendentals=0
        ),
        name="reorder",
    )(inverse, array)


def swap(array, axes):
    return lax.all_to_all(array, axes, split_axis=0, concat_axis=0, tiled=True)


def split_kernel(source, *refs):
    outs, sem = refs[:3], refs[3]
    copies = [
        pltpu.make_async_copy(source.at[:, k], out, sem.at[k])
        for k, out in enumerate(outs)
    ]
    for copy in copies:
        copy.start()
    for copy in copies:
        copy.wait()


def split(moved):
    count, _, piece, columns = moved.shape
    return pl.pallas_call(
        split_kernel,
        in_specs=[held()],
        out_specs=[pl.BlockSpec(memory_space=pl.ANY)] * 3,
        out_shape=[jax.ShapeDtypeStruct((count, piece, columns), BF)] * 3,
        scratch_shapes=[pltpu.SemaphoreType.DMA((3,))],
        compiler_params=pltpu.CompilerParams(vmem_limit_bytes=4 * MIB),
        cost_estimate=pl.CostEstimate(flops=0, bytes_accessed=4 * moved.size, transcendentals=0),
        name="split",
    )(moved)


def local(tokens, cotangent, gate_probs, routes, placement, weights, first_moment, second_moment):
    experts = lax.axis_size("expert")
    tok, width = tokens.shape
    top = routes.shape[1]
    cap = max(2, (3 * tok * top + 2 * experts - 1) // (2 * experts))
    rank = lax.axis_index("dp")
    weight = weights[0]
    rows = weight.shape[0] // 2
    piece = rows // (2 * experts)
    columns = weight.shape[1]
    both = ("expert", "dp")
    together = lax.optimization_barrier

    place = rank.reshape(1).astype(jnp.int32)
    labels = jnp.arange(experts, dtype=jnp.int32)
    inverse = jnp.sum(
        labels[None, :] * (placement[None, :] == labels[:, None]).astype(jnp.int32), axis=1
    )
    inverse = jnp.minimum(inverse, experts - 1)
    send = dispatch(routes.T, gate_probs.T, tokens, cotangent, experts, cap)
    send, inverse, place = together((send, inverse, place))
    recv = swap(send.reshape(-1, width // 4), both)
    weight = weight.reshape(2, 2, rows // 2, columns)
    recv, inverse, place = together((recv, inverse, place))
    own0, out0 = front_call(place, recv, weight, cap, 0)
    own1, out1 = front_call(place, recv, weight, cap, 1)
    other = [lax.ppermute(out, "dp", [(0, 1), (1, 0)]) for out in (out0, out1)]
    recv, own1 = together((recv, own1))
    x, c = sort_call(recv, cap)
    sent = rear_call(
        place, x, c, [own0, own1], other, weight, first_moment[0], second_moment[0], cap, piece
    )
    sent, inverse = together((sent, inverse))
    back = swap(sent.reshape(-1, columns), both).reshape(sent.shape)
    ready = reorder(back, inverse)
    mixed, token_grad = combine(routes.T, gate_probs.T, back, experts, cap)
    ready, mixed, token_grad = together((ready, mixed, token_grad))
    moved = swap(ready.reshape(-1, columns), both).reshape(ready.shape)
    m, v, step = (array.reshape(1, rows, columns) for array in split(moved))
    return (mixed, token_grad, m, v, step)


def solution(mesh):
    in_specs = (
        P(("expert", "dp"), None),
        P(("expert", "dp"), None),
        P(("expert", "dp"), None),
        P(("expert", "dp"), None),
        P(),
        P("expert", None, None),
        P("expert", "dp", None),
        P("expert", "dp", None),
    )
    out_specs = (
        P(("expert", "dp"), None),
        P(("expert", "dp"), None),
        P("expert", "dp", None),
        P("expert", "dp", None),
        P("expert", "dp", None),
    )
    return jax.shard_map(local, mesh=mesh, in_specs=in_specs, out_specs=out_specs, check_vma=False)
```

```python
import functools
import jax
import jax.numpy as jnp
from jax import lax
from jax.experimental import pallas as pl
from jax.experimental.pallas import tpu as pltpu
from jax.sharding import PartitionSpec as P

BF = jnp.bfloat16
F32 = jnp.float32
MIB = 1024 * 1024
DISPATCH_VMEM, FRONT_VMEM, SORT_VMEM = 20 * MIB, 12 * MIB, 12 * MIB
REAR_VMEM, COMBINE_VMEM = 12 * MIB, 16 * MIB
TILE = 512


def slots_of(route, experts, cap):
    tok = route.shape[1]
    label = lax.broadcasted_iota(jnp.int32, (experts, tok), 0)
    one0 = jnp.where(label == route[0:1, :], 1.0, 0.0)
    one1 = jnp.where(label == route[1:2, :], 1.0, 0.0)
    before = lax.broadcasted_iota(jnp.int32, (tok, tok), 0) < lax.broadcasted_iota(
        jnp.int32, (tok, tok), 1
    )
    count = jnp.dot(
        (one0 + one1).astype(BF),
        jnp.where(before, 1.0, 0.0).astype(BF),
        preferred_element_type=F32,
    )
    earlier0 = jnp.sum(one0 * count, axis=0, keepdims=True).astype(jnp.int32)
    earlier1 = jnp.sum(one1 * count, axis=0, keepdims=True).astype(jnp.int32)
    return route[0:1, :] * cap + earlier0, route[1:2, :] * cap + earlier1


def dispatch_kernel(
    cap, experts, route_ref, prob_ref, token_ref, cot_ref, out_ref, rows_in, low, high, scale,
    route, probs, sem
):
    tok, width = token_ref.shape
    per = 4 * cap
    small = [
        pltpu.make_async_copy(route_ref, route, sem.at[2]),
        pltpu.make_async_copy(prob_ref, probs, sem.at[3]),
    ]
    loads = [
        pltpu.make_async_copy(token_ref, rows_in.at[pl.ds(0, tok), :], sem.at[0]),
        pltpu.make_async_copy(cot_ref, rows_in.at[pl.ds(tok, tok), :], sem.at[1]),
    ]
    for load in small + loads:
        load.start()
    for load in small:
        load.wait()
    slot0, slot1 = slots_of(route[...], experts, cap)
    reach = 2 * per // 3
    shape = (experts, reach, tok)
    for half, ref in ((0, low), (1, high)):
        at = lax.broadcasted_iota(jnp.int32, shape, 1) + half * (reach // 2 - 2 * cap)
        ok = (at >= 0) & (at < 2 * cap)
        a = jnp.where(at >= cap, 1, 0)
        ident = lax.broadcasted_iota(jnp.int32, shape, 0) * cap + at - cap * a
        ident = jnp.where(ok, ident, -1).reshape(experts * reach, tok)
        a = a.reshape(experts * reach, tok)
        hit0 = ident == slot0
        hit1 = ident == slot1
        hit = hit0 | hit1
        for kind in (0, 1):
            ref[:, kind * tok : (kind + 1) * tok] = jnp.where(
                hit & (a == kind), 1.0, 0.0
            ).astype(BF)
        prob = jnp.where(hit0, probs[0:1, :], 0.0) + jnp.where(hit1, probs[1:2, :], 0.0)
        prob = jnp.sum(prob, axis=1, keepdims=True)
        scale[half] = jnp.where(a == 0, 1.0, prob)
    for load in loads:
        load.wait()
    half_width = width // 4
    lot = 16


    def body(i, carry):
        for r in range(2):
            first, second = (
                rows_in[
                    :, pl.ds(pl.multiple_of((2 * r + h) * half_width + i * TILE, TILE), TILE)
                ]
                for h in range(2)
            )
            at = pl.ds(pl.multiple_of(i * TILE, TILE), TILE)
            for g in range(experts // lot):
                part = slice(g * lot * reach, (g + 1) * lot * reach)
                y0 = jnp.dot(low[part, :], first, preferred_element_type=F32)
                y1 = jnp.dot(high[part, :], second, preferred_element_type=F32)
                y0 = y0 * scale[0, part, 0:1]
                y1 = y1 * scale[1, part, 0:1]
                mid = reach // 2
                for j in range(lot):
                    base = j * reach
                    made = [
                        y0[base : base + mid],
                        y0[base + mid : base + reach] + y1[base : base + mid],
                        y1[base + mid : base + reach],
                    ]
                    out_ref[g * lot + j, r, :, at] = jnp.concatenate(made, axis=0).astype(BF)
        return carry

    lax.fori_loop(0, half_width // TILE, body, 0)


def dispatch(routes, probs, tokens, cotangent, experts, cap):
    tok, width = tokens.shape
    half = width // 4
    per = 4 * cap
    rows = experts * per * 2 // 3
    anywhere = pl.BlockSpec(memory_space=pl.ANY)
    return pl.pallas_call(
        functools.partial(dispatch_kernel, cap, experts),
        in_specs=[anywhere] * 4,
        out_specs=held(),
        out_shape=jax.ShapeDtypeStruct((experts, 2, per, half), BF),
        scratch_shapes=[
            pltpu.VMEM((2 * tok, width), BF),
            pltpu.VMEM((rows, 2 * tok), BF),
            pltpu.VMEM((rows, 2 * tok), BF),
            pltpu.VMEM((2, rows, 128), F32),
            pltpu.VMEM((2, tok), jnp.int32),
            pltpu.VMEM((2, tok), F32),
            pltpu.SemaphoreType.DMA((4,)),
        ],
        compiler_params=pltpu.CompilerParams(vmem_limit_bytes=DISPATCH_VMEM),
        cost_estimate=pl.CostEstimate(
            flops=3 * 10**9, bytes_accessed=13 * MIB, transcendentals=0
        ),
        name="dispatch",
    )(routes, probs, tokens, cotangent)


def order_matrix(group, cap, inverse, paired=False):
    n = group * cap * 4
    i = lax.broadcasted_iota(jnp.int32, (n, n), 1 if inverse else 0)
    j = lax.broadcasted_iota(jnp.int32, (n, n), 0 if inverse else 1)
    hk = i // (group * cap)
    rest = i - hk * (group * cap)
    src = rest // cap
    slot = rest - src * cap
    if paired:
        part = src // (group // 2)
        src = 2 * (src - part * (group // 2)) + part
    return jnp.where(src * (4 * cap) + hk * cap + slot == j, 1.0, 0.0).astype(BF)


def unmix(fore, recv_ref, first, columns, group, cap):
    n = group * cap
    span = 4 * n
    made = [[] for _ in range(4)]
    for g in range(first.stop // span - first.start // span):
        rows = slice(first.start + g * span, first.start + (g + 1) * span)
        got = jnp.dot(
            fore, recv_ref[rows, columns], preferred_element_type=F32
        ).astype(BF)
        for k in range(4):
            made[k].append(got[k * n : (k + 1) * n])
    return made


def front_kernel(cap, group, part, rank_ref, recv_ref, w_ref, sum_ref, send_ref):
    total = recv_ref.shape[0] // 2
    columns = sum_ref.shape[1]
    front = columns // 3 * 2
    rank = rank_ref[0]
    fore = order_matrix(group, cap, False)
    sum_ref[...] = jnp.zeros_like(sum_ref)

    def body(i, carry):
        at = pl.ds(pl.multiple_of(i * TILE, TILE), TILE)
        made = unmix(fore, recv_ref, slice(part * total, (part + 1) * total), at, group, cap)
        for h in range(2):
            x = jnp.concatenate(made[2 * h], axis=0)
            c = jnp.concatenate(made[2 * h + 1], axis=0)
            w = w_ref[rank, h, at, :]
            sum_ref[:, :front] += jnp.dot(x, w[:, :front], preferred_element_type=F32)
            sum_ref[:, front:] += jnp.dot(c, w[:, front:], preferred_element_type=F32)
        return carry

    lax.fori_loop(0, recv_ref.shape[1] // TILE, body, 0)
    send_ref[...] = sum_ref[...].astype(BF)


def sort_kernel(cap, group, recv_ref, x_ref, c_ref):
    n = group * cap
    fore = order_matrix(group, cap, False)

    def body(i, carry):
        at = pl.ds(pl.multiple_of(i * TILE, TILE), TILE)
        made = unmix(fore, recv_ref, slice(0, recv_ref.shape[0]), at, group, cap)
        for g in range(len(made[0])):
            rows = slice(g * n, (g + 1) * n)
            for h in range(2):
                x_ref[h, rows, at] = made[2 * h][g]
                c_ref[h, rows, at] = made[2 * h + 1][g]
        return carry

    lax.fori_loop(0, recv_ref.shape[1] // TILE, body, 0)


GROUP = 8


def held():
    return pl.BlockSpec(memory_space=pltpu.VMEM)


def scalars():
    return pl.BlockSpec(memory_space=pltpu.SMEM)


def front_call(rank, recv, weight, cap, part):
    total, half = recv.shape
    columns = weight.shape[-1]
    rows = total // 8
    return pl.pallas_call(
        functools.partial(front_kernel, cap, GROUP, part),
        in_specs=[scalars(), held(), held()],
        out_specs=[held(), held()],
        out_shape=[
            jax.ShapeDtypeStruct((rows, columns), F32),
            jax.ShapeDtypeStruct((rows, columns), BF),
        ],
        compiler_params=pltpu.CompilerParams(vmem_limit_bytes=FRONT_VMEM),
        cost_estimate=pl.CostEstimate(
            flops=2 * 10**9, bytes_accessed=7 * MIB, transcendentals=0
        ),
        name="expert_front",
    )(rank, recv, weight)


def sort_call(recv, cap):
    total, half = recv.shape
    rows = total // 4
    return pl.pallas_call(
        functools.partial(sort_kernel, cap, GROUP),
        in_specs=[held()],
        out_specs=[held(), held()],
        out_shape=[jax.ShapeDtypeStruct((2, rows, half), BF)] * 2,
        compiler_params=pltpu.CompilerParams(vmem_limit_bytes=SORT_VMEM),
        cost_estimate=pl.CostEstimate(
            flops=2 * 10**9, bytes_accessed=19 * MIB, transcendentals=0
        ),
        name="sort_rows",
    )(recv)


def rear_kernel(
    cap, group, piece, rank_ref, x_ref, c_ref, own0, own1, other0, other1, w_ref, first_ref,
    second_ref, out_ref, inner, pre
):
    n = group * cap
    per = 4 * cap
    sets = out_ref.shape[0] // group
    tiles, tile = out_ref.shape[1] - 3, out_ref.shape[3]
    hidden = inner.shape[1]
    rank = rank_ref[0]
    back = order_matrix(group, cap, True)
    total = jnp.concatenate(
        [own0[...] + other0[...].astype(F32), own1[...] + other1[...].astype(F32)], axis=0
    )
    gate = total[:, :hidden]
    up = total[:, hidden : 2 * hidden]
    grad = total[:, 2 * hidden :]
    sig = jax.nn.sigmoid(gate)
    active = gate * sig
    inner[...] = (active * up).astype(BF)
    slope = sig * (1.0 + gate * (1.0 - sig))
    pre[:, :hidden] = (grad * up * slope).astype(BF)
    pre[:, hidden:] = (grad * active).astype(BF)
    contract = (((1,), (1,)), ((), ()))
    lead = (((0,), (0,)), ((), ()))

    def body(i, carry):
        cols = pl.ds(pl.multiple_of(i * tile, tile), tile)
        made = []
        for h in range(2):
            for factor, at in (
                (inner, slice(2 * hidden, 3 * hidden)),
                (pre, slice(0, 2 * hidden)),
            ):
                made.append(
                    lax.dot_general(
                        factor[...], w_ref[rank, h, cols, at], contract,
                        preferred_element_type=F32,
                    ).astype(BF)
                )
        for g in range(sets):
            stack = jnp.concatenate([m[g * n : (g + 1) * n] for m in made], axis=0)
            mixed = jnp.dot(back, stack, preferred_element_type=F32)
            for j in range(group):
                out_ref[g * group + j, i] = mixed[j * per : (j + 1) * per].astype(BF)
        for h in range(2):
            for source, factor, at in (
                (x_ref, pre, slice(0, 2 * hidden)),
                (c_ref, inner, slice(2 * hidden, 3 * hidden)),
            ):
                grad = lax.dot_general(
                    source[h, :, cols], factor[...], lead, preferred_element_type=F32
                )
                m = 0.9 * first_ref[h, cols, at].astype(F32) + 0.1 * grad
                v = 0.95 * second_ref[h, cols, at].astype(F32) + 0.05 * grad * grad
                step = m / (jnp.sqrt(v) + 1e-08) + 0.1 * w_ref[rank, h, cols, at].astype(F32)
                count = tile // piece
                for k, value in enumerate((m, v, step)):
                    for j in range(count):
                        out_ref[(h * tiles + i) * count + j, tiles + k, :, at] = value[
                            j * piece : (j + 1) * piece
                        ].astype(BF)
        return carry

    lax.fori_loop(0, tiles, body, 0)


def rear_call(rank, x, c, own, other, weight, first, second, cap, piece):
    rows, half = x.shape[1:]
    columns = weight.shape[-1]
    hidden = columns // 3
    tile = 3 * hidden
    tiles = half // tile
    return pl.pallas_call(
        functools.partial(rear_kernel, cap, GROUP, piece),
        in_specs=[scalars()] + [held()] * 9,
        out_specs=held(),
        scratch_shapes=[pltpu.VMEM((rows, hidden), BF), pltpu.VMEM((rows, 2 * hidden), BF)],
        out_shape=jax.ShapeDtypeStruct((rows // cap, tiles + 3, piece, tile), BF),
        compiler_params=pltpu.CompilerParams(vmem_limit_bytes=REAR_VMEM),
        cost_estimate=pl.CostEstimate(
            flops=7 * 10**9, bytes_accessed=36 * MIB, transcendentals=rows * hidden
        ),
        name="expert_rear",
    )(
        rank, x, c, *own, *other, weight,
        first.reshape(2, half, columns), second.reshape(2, half, columns),
    )


def column(row):
    n = row.shape[1]
    same = lax.broadcasted_iota(jnp.int32, (n, n), 0) == lax.broadcasted_iota(
        jnp.int32, (n, n), 1
    )
    return jnp.sum(jnp.where(same, row, jnp.zeros_like(row)), axis=1, keepdims=True)


def combine_kernel(
    cap, group, experts, route_ref, prob_ref, back_ref, mixed_ref, grad_ref, stage, pick, both,
    mixed, grads, sem
):
    sources, _, per, tile = back_ref.shape
    tok, width = mixed.shape
    half = width // 4
    tiles = half // tile
    m = group // 2 * cap
    rows = experts * cap
    fore = order_matrix(group, cap, False, True)
    slot0, slot1 = slots_of(route_ref[...], experts, cap)
    prob0, prob1 = column(prob_ref[0:1, :]), column(prob_ref[1:2, :])
    ident = lax.broadcasted_iota(jnp.int32, (tok, rows), 1)
    hit0 = ident == column(slot0)
    hit1 = ident == column(slot1)
    pick[:tok, :] = jnp.where(hit0, 1.0, 0.0).astype(BF)
    pick[tok:, :] = jnp.where(hit1, 1.0, 0.0).astype(BF)
    both[...] = jnp.where(hit0 | hit1, 1.0, 0.0).astype(BF)
    sends = []
    for i in range(tiles):
        for g in range(sources // group):
            block = back_ref[g * group : (g + 1) * group, i].reshape(group * per, tile)
            got = jnp.dot(fore, block, preferred_element_type=F32)
            for k in range(4):
                for r in range(2):
                    at = (2 * k + r) * m
                    stage[k, r, g * m : (g + 1) * m, :] = got[at : at + m].astype(BF)
        for r in range(2):
            for h in range(2):
                to = slice((2 * r + h) * half + i * tile, (2 * r + h) * half + (i + 1) * tile)
                out = jnp.dot(pick[...], stage[2 * h, r], preferred_element_type=F32)
                grad = jnp.dot(both[...], stage[2 * h + 1, r], preferred_element_type=F32)
                mixed[:, to] = (out[:tok] * prob0 + out[tok:] * prob1).astype(BF)
                grads[:, to] = grad.astype(BF)
                for k, (source, target) in enumerate(((mixed, mixed_ref), (grads, grad_ref))):
                    at = pl.ds(to.start, tile)
                    send = pltpu.make_async_copy(
                        source.at[:, at], target.at[:, at], sem.at[k, len(sends) // 2]
                    )
                    send.start()
                    sends.append(send)
    for send in sends:
        send.wait()


def combine(routes, probs, back, experts, cap):
    sources, slabs, _, tile = back.shape
    rows = experts * cap
    tok = routes.shape[1]
    width = 4 * (slabs - 3) * tile
    shape = jax.ShapeDtypeStruct((tok, width), BF)
    return pl.pallas_call(
        functools.partial(combine_kernel, cap, GROUP, experts),
        in_specs=[held()] * 3,
        out_specs=[pl.BlockSpec(memory_space=pl.ANY)] * 2,
        out_shape=[shape, shape],
        scratch_shapes=[
            pltpu.VMEM((4, 2, rows, tile), BF),
            pltpu.VMEM((2 * tok, rows), BF),
            pltpu.VMEM((tok, rows), BF),
            pltpu.VMEM((tok, width), BF),
            pltpu.VMEM((tok, width), BF),
            pltpu.SemaphoreType.DMA((2, width // tile)),
        ],
        compiler_params=pltpu.CompilerParams(vmem_limit_bytes=COMBINE_VMEM),
        cost_estimate=pl.CostEstimate(
            flops=6 * 10**9, bytes_accessed=13 * MIB, transcendentals=0
        ),
        name="combine",
    )(routes, probs, back)


def reorder_kernel(place_ref, source, out):
    def body(e, carry):
        for r in range(2):
            out[2 * place_ref[e] + r] = source[2 * e + r, -3:]
        return carry

    lax.fori_loop(0, out.shape[0] // 2, body, 0)


def reorder(array, placement):
    sources, _, piece, columns = array.shape
    return pl.pallas_call(
        reorder_kernel,
        in_specs=[scalars(), held()],
        out_specs=held(),
        out_shape=jax.ShapeDtypeStruct((sources, 3, piece, columns), BF),
        compiler_params=pltpu.CompilerParams(vmem_limit_bytes=4 * MIB),
        cost_estimate=pl.CostEstimate(
            flops=0, bytes_accessed=12 * sources * piece * columns, transcendentals=0
        ),
        name="reorder",
    )(placement, array)


def swap(array, axes):
    return lax.all_to_all(array, axes, split_axis=0, concat_axis=0, tiled=True)


def split_kernel(source, *refs):
    outs, sem = refs[:3], refs[3]
    copies = [
        pltpu.make_async_copy(source.at[:, k], out, sem.at[k])
        for k, out in enumerate(outs)
    ]
    for copy in copies:
        copy.start()
    for copy in copies:
        copy.wait()


def split(moved):
    count, _, piece, columns = moved.shape
    return pl.pallas_call(
        split_kernel,
        in_specs=[held()],
        out_specs=[pl.BlockSpec(memory_space=pl.ANY)] * 3,
        out_shape=[jax.ShapeDtypeStruct((count, piece, columns), BF)] * 3,
        scratch_shapes=[pltpu.SemaphoreType.DMA((3,))],
        compiler_params=pltpu.CompilerParams(vmem_limit_bytes=4 * MIB),
        cost_estimate=pl.CostEstimate(flops=0, bytes_accessed=4 * moved.size, transcendentals=0),
        name="split",
    )(moved)


def local(tokens, cotangent, gate_probs, routes, placement, weights, first_moment, second_moment):
    experts = lax.axis_size("expert")
    tok, width = tokens.shape
    top = routes.shape[1]
    cap = max(2, (3 * tok * top + 2 * experts - 1) // (2 * experts))
    rank = lax.axis_index("dp")
    weight = weights[0]
    rows = weight.shape[0] // 2
    piece = rows // (2 * experts)
    columns = weight.shape[1]
    both = ("expert", "dp")
    together = lax.optimization_barrier

    place = rank.reshape(1).astype(jnp.int32)
    send = dispatch(routes.T, gate_probs.T, tokens, cotangent, experts, cap)
    send, place = together((send, place))
    recv = swap(send.reshape(-1, width // 4), both)
    weight = weight.reshape(2, 2, rows // 2, columns)
    recv, place = together((recv, place))
    own0, out0 = front_call(place, recv, weight, cap, 0)
    own1, out1 = front_call(place, recv, weight, cap, 1)
    other = [lax.ppermute(out, "dp", [(0, 1), (1, 0)]) for out in (out0, out1)]
    recv, own1 = together((recv, own1))
    x, c = sort_call(recv, cap)
    sent = rear_call(
        place, x, c, [own0, own1], other, weight, first_moment[0], second_moment[0], cap, piece
    )
    back = swap(sent.reshape(-1, columns), both).reshape(sent.shape)
    ready = reorder(back, placement)
    mixed, token_grad = combine(routes.T, gate_probs.T, back, experts, cap)
    ready, mixed, token_grad = together((ready, mixed, token_grad))
    moved = swap(ready.reshape(-1, columns), both).reshape(ready.shape)
    m, v, step = (array.reshape(1, rows, columns) for array in split(moved))
    return (mixed, token_grad, m, v, step)


def solution(mesh):
    in_specs = (
        P(("expert", "dp"), None),
        P(("expert", "dp"), None),
        P(("expert", "dp"), None),
        P(("expert", "dp"), None),
        P(),
        P("expert", None, None),
        P("expert", "dp", None),
        P("expert", "dp", None),
    )
    out_specs = (
        P(("expert", "dp"), None),
        P(("expert", "dp"), None),
        P("expert", "dp", None),
        P("expert", "dp", None),
        P("expert", "dp", None),
    )
    return jax.shard_map(local, mesh=mesh, in_specs=in_specs, out_specs=out_specs, check_vma=False)
```

```python
import functools
import jax
import jax.numpy as jnp
from jax import lax
from jax.experimental import pallas as pl
from jax.experimental.pallas import tpu as pltpu
from jax.sharding import PartitionSpec as P

BF = jnp.bfloat16
F32 = jnp.float32
MIB = 1024 * 1024
DISPATCH_VMEM, FRONT_VMEM, SORT_VMEM = 20 * MIB, 12 * MIB, 12 * MIB
REAR_VMEM, COMBINE_VMEM = 12 * MIB, 16 * MIB
TILE = 512


def slots_of(route, experts, cap):
    tok = route.shape[1]
    label = lax.broadcasted_iota(jnp.int32, (experts, tok), 0)
    one0 = jnp.where(label == route[0:1, :], 1.0, 0.0)
    one1 = jnp.where(label == route[1:2, :], 1.0, 0.0)
    before = lax.broadcasted_iota(jnp.int32, (tok, tok), 0) < lax.broadcasted_iota(
        jnp.int32, (tok, tok), 1
    )
    count = jnp.dot(
        (one0 + one1).astype(BF),
        jnp.where(before, 1.0, 0.0).astype(BF),
        preferred_element_type=F32,
    )
    earlier0 = jnp.sum(one0 * count, axis=0, keepdims=True).astype(jnp.int32)
    earlier1 = jnp.sum(one1 * count, axis=0, keepdims=True).astype(jnp.int32)
    return route[0:1, :] * cap + earlier0, route[1:2, :] * cap + earlier1


def dispatch_kernel(
    cap, experts, route_ref, prob_ref, token_ref, cot_ref, out_ref, rows_in, low, high, scale,
    route, probs, sem
):
    tok, width = token_ref.shape
    per = 4 * cap
    small = [
        pltpu.make_async_copy(route_ref, route, sem.at[2]),
        pltpu.make_async_copy(prob_ref, probs, sem.at[3]),
    ]
    loads = [
        pltpu.make_async_copy(token_ref, rows_in.at[pl.ds(0, tok), :], sem.at[0]),
        pltpu.make_async_copy(cot_ref, rows_in.at[pl.ds(tok, tok), :], sem.at[1]),
    ]
    for load in small + loads:
        load.start()
    for load in small:
        load.wait()
    slot0, slot1 = slots_of(route[...], experts, cap)
    reach = 2 * per // 3
    shape = (experts, reach, tok)
    for half, ref in ((0, low), (1, high)):
        at = lax.broadcasted_iota(jnp.int32, shape, 1) + half * (reach // 2 - 2 * cap)
        ok = (at >= 0) & (at < 2 * cap)
        a = jnp.where(at >= cap, 1, 0)
        ident = lax.broadcasted_iota(jnp.int32, shape, 0) * cap + at - cap * a
        ident = jnp.where(ok, ident, -1).reshape(experts * reach, tok)
        a = a.reshape(experts * reach, tok)
        hit0 = ident == slot0
        hit1 = ident == slot1
        hit = hit0 | hit1
        for kind in (0, 1):
            ref[:, kind * tok : (kind + 1) * tok] = jnp.where(
                hit & (a == kind), 1.0, 0.0
            ).astype(BF)
        prob = jnp.where(hit0, probs[0:1, :], 0.0) + jnp.where(hit1, probs[1:2, :], 0.0)
        prob = jnp.sum(prob, axis=1, keepdims=True)
        scale[half] = jnp.where(a == 0, 1.0, prob)
    for load in loads:
        load.wait()
    half_width = width // 4
    lot = 16


    def body(i, carry):
        for r in range(2):
            first, second = (
                rows_in[
                    :, pl.ds(pl.multiple_of((2 * r + h) * half_width + i * TILE, TILE), TILE)
                ]
                for h in range(2)
            )
            at = pl.ds(pl.multiple_of(i * TILE, TILE), TILE)
            for g in range(experts // lot):
                part = slice(g * lot * reach, (g + 1) * lot * reach)
                y0 = jnp.dot(low[part, :], first, preferred_element_type=F32)
                y1 = jnp.dot(high[part, :], second, preferred_element_type=F32)
                y0 = y0 * scale[0, part, 0:1]
                y1 = y1 * scale[1, part, 0:1]
                mid = reach // 2
                for j in range(lot):
                    base = j * reach
                    made = [
                        y0[base : base + mid],
                        y0[base + mid : base + reach] + y1[base : base + mid],
                        y1[base + mid : base + reach],
                    ]
                    out_ref[g * lot + j, r, :, at] = jnp.concatenate(made, axis=0).astype(BF)
        return carry

    lax.fori_loop(0, half_width // TILE, body, 0)


def dispatch(routes, probs, tokens, cotangent, experts, cap):
    tok, width = tokens.shape
    half = width // 4
    per = 4 * cap
    rows = experts * per * 2 // 3
    anywhere = pl.BlockSpec(memory_space=pl.ANY)
    return pl.pallas_call(
        functools.partial(dispatch_kernel, cap, experts),
        in_specs=[anywhere] * 4,
        out_specs=held(),
        out_shape=jax.ShapeDtypeStruct((experts, 2, per, half), BF),
        scratch_shapes=[
            pltpu.VMEM((2 * tok, width), BF),
            pltpu.VMEM((rows, 2 * tok), BF),
            pltpu.VMEM((rows, 2 * tok), BF),
            pltpu.VMEM((2, rows, 128), F32),
            pltpu.VMEM((2, tok), jnp.int32),
            pltpu.VMEM((2, tok), F32),
            pltpu.SemaphoreType.DMA((4,)),
        ],
        compiler_params=pltpu.CompilerParams(vmem_limit_bytes=DISPATCH_VMEM),
        cost_estimate=pl.CostEstimate(
            flops=3 * 10**9, bytes_accessed=13 * MIB, transcendentals=0
        ),
        name="dispatch",
    )(routes, probs, tokens, cotangent)


def order_matrix(group, cap, inverse, paired=False):
    n = group * cap * 4
    i = lax.broadcasted_iota(jnp.int32, (n, n), 1 if inverse else 0)
    j = lax.broadcasted_iota(jnp.int32, (n, n), 0 if inverse else 1)
    hk = i // (group * cap)
    rest = i - hk * (group * cap)
    src = rest // cap
    slot = rest - src * cap
    if paired:
        part = src // (group // 2)
        src = 2 * (src - part * (group // 2)) + part
    return jnp.where(src * (4 * cap) + hk * cap + slot == j, 1.0, 0.0).astype(BF)


def unmix(fore, recv_ref, first, columns, group, cap):
    n = group * cap
    span = 4 * n
    made = [[] for _ in range(4)]
    for g in range(first.stop // span - first.start // span):
        rows = slice(first.start + g * span, first.start + (g + 1) * span)
        got = jnp.dot(
            fore, recv_ref[rows, columns], preferred_element_type=F32
        ).astype(BF)
        for k in range(4):
            made[k].append(got[k * n : (k + 1) * n])
    return made


def front_kernel(cap, group, part, rank_ref, recv_ref, w_ref, sum_ref, send_ref):
    total = recv_ref.shape[0] // 2
    columns = sum_ref.shape[1]
    front = columns // 3 * 2
    rank = rank_ref[0]
    fore = order_matrix(group, cap, False)
    sum_ref[...] = jnp.zeros_like(sum_ref)

    def body(i, carry):
        at = pl.ds(pl.multiple_of(i * TILE, TILE), TILE)
        made = unmix(fore, recv_ref, slice(part * total, (part + 1) * total), at, group, cap)
        for h in range(2):
            x = jnp.concatenate(made[2 * h], axis=0)
            c = jnp.concatenate(made[2 * h + 1], axis=0)
            w = w_ref[rank, h, at, :]
            sum_ref[:, :front] += jnp.dot(x, w[:, :front], preferred_element_type=F32)
            sum_ref[:, front:] += jnp.dot(c, w[:, front:], preferred_element_type=F32)
        return carry

    lax.fori_loop(0, recv_ref.shape[1] // TILE, body, 0)
    send_ref[...] = sum_ref[...].astype(BF)


def sort_kernel(cap, group, recv_ref, x_ref, c_ref):
    n = group * cap
    fore = order_matrix(group, cap, False)

    def body(i, carry):
        at = pl.ds(pl.multiple_of(i * TILE, TILE), TILE)
        made = unmix(fore, recv_ref, slice(0, recv_ref.shape[0]), at, group, cap)
        for g in range(len(made[0])):
            rows = slice(g * n, (g + 1) * n)
            for h in range(2):
                x_ref[h, rows, at] = made[2 * h][g]
                c_ref[h, rows, at] = made[2 * h + 1][g]
        return carry

    lax.fori_loop(0, recv_ref.shape[1] // TILE, body, 0)


GROUP = 8


def held():
    return pl.BlockSpec(memory_space=pltpu.VMEM)


def scalars():
    return pl.BlockSpec(memory_space=pltpu.SMEM)


def front_call(rank, recv, weight, cap, part):
    total, half = recv.shape
    columns = weight.shape[-1]
    rows = total // 8
    return pl.pallas_call(
        functools.partial(front_kernel, cap, GROUP, part),
        in_specs=[scalars(), held(), held()],
        out_specs=[held(), held()],
        out_shape=[
            jax.ShapeDtypeStruct((rows, columns), F32),
            jax.ShapeDtypeStruct((rows, columns), BF),
        ],
        compiler_params=pltpu.CompilerParams(vmem_limit_bytes=FRONT_VMEM),
        cost_estimate=pl.CostEstimate(
            flops=2 * 10**9, bytes_accessed=7 * MIB, transcendentals=0
        ),
        name="expert_front",
    )(rank, recv, weight)


def sort_call(recv, cap):
    total, half = recv.shape
    rows = total // 4
    return pl.pallas_call(
        functools.partial(sort_kernel, cap, GROUP),
        in_specs=[held()],
        out_specs=[held(), held()],
        out_shape=[jax.ShapeDtypeStruct((2, rows, half), BF)] * 2,
        compiler_params=pltpu.CompilerParams(vmem_limit_bytes=SORT_VMEM),
        cost_estimate=pl.CostEstimate(
            flops=2 * 10**9, bytes_accessed=19 * MIB, transcendentals=0
        ),
        name="sort_rows",
    )(recv)


def rear_kernel(
    cap, group, piece, rank_ref, x_ref, c_ref, own0, own1, other0, other1, w_ref, first_ref,
    second_ref, out_ref, inner, pre
):
    n = group * cap
    per = 4 * cap
    sets = out_ref.shape[0] // group
    tiles, tile = out_ref.shape[1] - 3, out_ref.shape[3]
    hidden = inner.shape[1]
    rank = rank_ref[0]
    back = order_matrix(group, cap, True)
    total = jnp.concatenate(
        [own0[...] + other0[...].astype(F32), own1[...] + other1[...].astype(F32)], axis=0
    )
    gate = total[:, :hidden]
    up = total[:, hidden : 2 * hidden]
    grad = total[:, 2 * hidden :]
    sig = jax.nn.sigmoid(gate)
    active = gate * sig
    inner[...] = (active * up).astype(BF)
    slope = sig * (1.0 + gate * (1.0 - sig))
    pre[:, :hidden] = (grad * up * slope).astype(BF)
    pre[:, hidden:] = (grad * active).astype(BF)
    contract = (((1,), (1,)), ((), ()))
    lead = (((0,), (0,)), ((), ()))

    def body(i, carry):
        cols = pl.ds(pl.multiple_of(i * tile, tile), tile)
        made = []
        for h in range(2):
            for factor, at in (
                (inner, slice(2 * hidden, 3 * hidden)),
                (pre, slice(0, 2 * hidden)),
            ):
                made.append(
                    lax.dot_general(
                        factor[...], w_ref[rank, h, cols, at], contract,
                        preferred_element_type=F32,
                    ).astype(BF)
                )
        for g in range(sets):
            stack = jnp.concatenate([m[g * n : (g + 1) * n] for m in made], axis=0)
            mixed = jnp.dot(back, stack, preferred_element_type=F32)
            for j in range(group):
                out_ref[g * group + j, i] = mixed[j * per : (j + 1) * per].astype(BF)
        for h in range(2):
            for source, factor, at in (
                (x_ref, pre, slice(0, 2 * hidden)),
                (c_ref, inner, slice(2 * hidden, 3 * hidden)),
            ):
                grad = lax.dot_general(
                    source[h, :, cols], factor[...], lead, preferred_element_type=F32
                )
                m = 0.9 * first_ref[h, cols, at].astype(F32) + 0.1 * grad
                v = 0.95 * second_ref[h, cols, at].astype(F32) + 0.05 * grad * grad
                scale = pl.reciprocal(v * lax.rsqrt(v) + 1e-08)
                step = m * scale + 0.1 * w_ref[rank, h, cols, at].astype(F32)
                count = tile // piece
                for k, value in enumerate((m, v, step)):
                    for j in range(count):
                        out_ref[(h * tiles + i) * count + j, tiles + k, :, at] = value[
                            j * piece : (j + 1) * piece
                        ].astype(BF)
        return carry

    lax.fori_loop(0, tiles, body, 0)


def rear_call(rank, x, c, own, other, weight, first, second, cap, piece):
    rows, half = x.shape[1:]
    columns = weight.shape[-1]
    hidden = columns // 3
    tile = 3 * hidden
    tiles = half // tile
    return pl.pallas_call(
        functools.partial(rear_kernel, cap, GROUP, piece),
        in_specs=[scalars()] + [held()] * 9,
        out_specs=held(),
        scratch_shapes=[pltpu.VMEM((rows, hidden), BF), pltpu.VMEM((rows, 2 * hidden), BF)],
        out_shape=jax.ShapeDtypeStruct((rows // cap, tiles + 3, piece, tile), BF),
        compiler_params=pltpu.CompilerParams(vmem_limit_bytes=REAR_VMEM),
        cost_estimate=pl.CostEstimate(
            flops=7 * 10**9, bytes_accessed=36 * MIB, transcendentals=rows * hidden
        ),
        name="expert_rear",
    )(
        rank, x, c, *own, *other, weight,
        first.reshape(2, half, columns), second.reshape(2, half, columns),
    )


def column(row):
    n = row.shape[1]
    same = lax.broadcasted_iota(jnp.int32, (n, n), 0) == lax.broadcasted_iota(
        jnp.int32, (n, n), 1
    )
    return jnp.sum(jnp.where(same, row, jnp.zeros_like(row)), axis=1, keepdims=True)


def combine_kernel(
    cap, group, experts, route_ref, prob_ref, back_ref, mixed_ref, grad_ref, stage, pick, both,
    mixed, grads, sem
):
    sources, _, per, tile = back_ref.shape
    tok, width = mixed.shape
    half = width // 4
    tiles = half // tile
    m = group // 2 * cap
    rows = experts * cap
    fore = order_matrix(group, cap, False, True)
    slot0, slot1 = slots_of(route_ref[...], experts, cap)
    prob0, prob1 = column(prob_ref[0:1, :]), column(prob_ref[1:2, :])
    ident = lax.broadcasted_iota(jnp.int32, (tok, rows), 1)
    hit0 = ident == column(slot0)
    hit1 = ident == column(slot1)
    pick[:tok, :] = jnp.where(hit0, 1.0, 0.0).astype(BF)
    pick[tok:, :] = jnp.where(hit1, 1.0, 0.0).astype(BF)
    both[...] = jnp.where(hit0 | hit1, 1.0, 0.0).astype(BF)
    sends = []
    for i in range(tiles):
        for g in range(sources // group):
            block = back_ref[g * group : (g + 1) * group, i].reshape(group * per, tile)
            got = jnp.dot(fore, block, preferred_element_type=F32)
            for k in range(4):
                for r in range(2):
                    at = (2 * k + r) * m
                    stage[k, r, g * m : (g + 1) * m, :] = got[at : at + m].astype(BF)
        for r in range(2):
            for h in range(2):
                to = slice((2 * r + h) * half + i * tile, (2 * r + h) * half + (i + 1) * tile)
                out = jnp.dot(pick[...], stage[2 * h, r], preferred_element_type=F32)
                grad = jnp.dot(both[...], stage[2 * h + 1, r], preferred_element_type=F32)
                mixed[:, to] = (out[:tok] * prob0 + out[tok:] * prob1).astype(BF)
                grads[:, to] = grad.astype(BF)
                for k, (source, target) in enumerate(((mixed, mixed_ref), (grads, grad_ref))):
                    at = pl.ds(to.start, tile)
                    send = pltpu.make_async_copy(
                        source.at[:, at], target.at[:, at], sem.at[k, len(sends) // 2]
                    )
                    send.start()
                    sends.append(send)
    for send in sends:
        send.wait()


def combine(routes, probs, back, experts, cap):
    sources, slabs, _, tile = back.shape
    rows = experts * cap
    tok = routes.shape[1]
    width = 4 * (slabs - 3) * tile
    shape = jax.ShapeDtypeStruct((tok, width), BF)
    return pl.pallas_call(
        functools.partial(combine_kernel, cap, GROUP, experts),
        in_specs=[held()] * 3,
        out_specs=[pl.BlockSpec(memory_space=pl.ANY)] * 2,
        out_shape=[shape, shape],
        scratch_shapes=[
            pltpu.VMEM((4, 2, rows, tile), BF),
            pltpu.VMEM((2 * tok, rows), BF),
            pltpu.VMEM((tok, rows), BF),
            pltpu.VMEM((tok, width), BF),
            pltpu.VMEM((tok, width), BF),
            pltpu.SemaphoreType.DMA((2, width // tile)),
        ],
        compiler_params=pltpu.CompilerParams(vmem_limit_bytes=COMBINE_VMEM),
        cost_estimate=pl.CostEstimate(
            flops=6 * 10**9, bytes_accessed=13 * MIB, transcendentals=0
        ),
        name="combine",
    )(routes, probs, back)


def reorder_kernel(place_ref, source, out):
    def body(e, carry):
        for r in range(2):
            out[2 * place_ref[e] + r] = source[2 * e + r, -3:]
        return carry

    lax.fori_loop(0, out.shape[0] // 2, body, 0)


def reorder(array, placement):
    sources, _, piece, columns = array.shape
    return pl.pallas_call(
        reorder_kernel,
        in_specs=[scalars(), held()],
        out_specs=held(),
        out_shape=jax.ShapeDtypeStruct((sources, 3, piece, columns), BF),
        compiler_params=pltpu.CompilerParams(vmem_limit_bytes=4 * MIB),
        cost_estimate=pl.CostEstimate(
            flops=0, bytes_accessed=12 * sources * piece * columns, transcendentals=0
        ),
        name="reorder",
    )(placement, array)


def swap(array, axes):
    return lax.all_to_all(array, axes, split_axis=0, concat_axis=0, tiled=True)


def split_kernel(source, *refs):
    outs, sem = refs[:3], refs[3]
    copies = [
        pltpu.make_async_copy(source.at[:, k], out, sem.at[k])
        for k, out in enumerate(outs)
    ]
    for copy in copies:
        copy.start()
    for copy in copies:
        copy.wait()


def split(moved):
    count, _, piece, columns = moved.shape
    return pl.pallas_call(
        split_kernel,
        in_specs=[held()],
        out_specs=[pl.BlockSpec(memory_space=pl.ANY)] * 3,
        out_shape=[jax.ShapeDtypeStruct((count, piece, columns), BF)] * 3,
        scratch_shapes=[pltpu.SemaphoreType.DMA((3,))],
        compiler_params=pltpu.CompilerParams(vmem_limit_bytes=4 * MIB),
        cost_estimate=pl.CostEstimate(flops=0, bytes_accessed=4 * moved.size, transcendentals=0),
        name="split",
    )(moved)


def local(tokens, cotangent, gate_probs, routes, placement, weights, first_moment, second_moment):
    experts = lax.axis_size("expert")
    tok, width = tokens.shape
    top = routes.shape[1]
    cap = max(2, (3 * tok * top + 2 * experts - 1) // (2 * experts))
    rank = lax.axis_index("dp")
    weight = weights[0]
    rows = weight.shape[0] // 2
    piece = rows // (2 * experts)
    columns = weight.shape[1]
    both = ("expert", "dp")
    together = lax.optimization_barrier

    place = rank.reshape(1).astype(jnp.int32)
    send = dispatch(routes.T, gate_probs.T, tokens, cotangent, experts, cap)
    send, place = together((send, place))
    recv = swap(send.reshape(-1, width // 4), both)
    weight = weight.reshape(2, 2, rows // 2, columns)
    recv, place = together((recv, place))
    own0, out0 = front_call(place, recv, weight, cap, 0)
    recv, own0 = together((recv, own0))
    x, c = sort_call(recv, cap)
    recv, x = together((recv, x))
    own1, out1 = front_call(place, recv, weight, cap, 1)
    other = [lax.ppermute(out, "dp", [(0, 1), (1, 0)]) for out in (out0, out1)]
    sent = rear_call(
        place, x, c, [own0, own1], other, weight, first_moment[0], second_moment[0], cap, piece
    )
    back = swap(sent.reshape(-1, columns), both).reshape(sent.shape)
    ready = reorder(back, placement)
    mixed, token_grad = combine(routes.T, gate_probs.T, back, experts, cap)
    ready, mixed, token_grad = together((ready, mixed, token_grad))
    moved = swap(ready.reshape(-1, columns), both).reshape(ready.shape)
    m, v, step = (array.reshape(1, rows, columns) for array in split(moved))
    return (mixed, token_grad, m, v, step)


def solution(mesh):
    in_specs = (
        P(("expert", "dp"), None),
        P(("expert", "dp"), None),
        P(("expert", "dp"), None),
        P(("expert", "dp"), None),
        P(),
        P("expert", None, None),
        P("expert", "dp", None),
        P("expert", "dp", None),
    )
    out_specs = (
        P(("expert", "dp"), None),
        P(("expert", "dp"), None),
        P("expert", "dp", None),
        P("expert", "dp", None),
        P("expert", "dp", None),
    )
    return jax.shard_map(local, mesh=mesh, in_specs=in_specs, out_specs=out_specs, check_vma=False)
```

```python
import functools
import jax
import jax.numpy as jnp
from jax import lax
from jax.experimental import pallas as pl
from jax.experimental.pallas import tpu as pltpu
from jax.sharding import PartitionSpec as P

BF = jnp.bfloat16
F32 = jnp.float32
MIB = 1024 * 1024
DISPATCH_VMEM, FRONT_VMEM, SORT_VMEM = 20 * MIB, 12 * MIB, 12 * MIB
REAR_VMEM, COMBINE_VMEM = 12 * MIB, 16 * MIB
TILE = 768


def slots_of(route, experts, cap):
    tok = route.shape[1]
    label = lax.broadcasted_iota(jnp.int32, (experts, tok), 0)
    one0 = jnp.where(label == route[0:1, :], 1.0, 0.0)
    one1 = jnp.where(label == route[1:2, :], 1.0, 0.0)
    before = lax.broadcasted_iota(jnp.int32, (tok, tok), 0) < lax.broadcasted_iota(
        jnp.int32, (tok, tok), 1
    )
    count = jnp.dot(
        (one0 + one1).astype(BF),
        jnp.where(before, 1.0, 0.0).astype(BF),
        preferred_element_type=F32,
    )
    earlier0 = jnp.sum(one0 * count, axis=0, keepdims=True).astype(jnp.int32)
    earlier1 = jnp.sum(one1 * count, axis=0, keepdims=True).astype(jnp.int32)
    return route[0:1, :] * cap + earlier0, route[1:2, :] * cap + earlier1


def dispatch_kernel(
    cap, experts, route_ref, prob_ref, token_ref, cot_ref, out_ref, rows_in, low, high, scale,
    route, probs, sem
):
    tok, width = token_ref.shape
    per = 4 * cap
    small = [
        pltpu.make_async_copy(route_ref, route, sem.at[2]),
        pltpu.make_async_copy(prob_ref, probs, sem.at[3]),
    ]
    loads = [
        pltpu.make_async_copy(token_ref, rows_in.at[pl.ds(0, tok), :], sem.at[0]),
        pltpu.make_async_copy(cot_ref, rows_in.at[pl.ds(tok, tok), :], sem.at[1]),
    ]
    for load in small + loads:
        load.start()
    for load in small:
        load.wait()
    slot0, slot1 = slots_of(route[...], experts, cap)
    reach = 2 * per // 3
    shape = (experts, reach, tok)
    for half, ref in ((0, low), (1, high)):
        at = lax.broadcasted_iota(jnp.int32, shape, 1) + half * (reach // 2 - 2 * cap)
        ok = (at >= 0) & (at < 2 * cap)
        a = jnp.where(at >= cap, 1, 0)
        ident = lax.broadcasted_iota(jnp.int32, shape, 0) * cap + at - cap * a
        ident = jnp.where(ok, ident, -1).reshape(experts * reach, tok)
        a = a.reshape(experts * reach, tok)
        hit0 = ident == slot0
        hit1 = ident == slot1
        hit = hit0 | hit1
        for kind in (0, 1):
            ref[:, kind * tok : (kind + 1) * tok] = jnp.where(
                hit & (a == kind), 1.0, 0.0
            ).astype(BF)
        prob = jnp.where(hit0, probs[0:1, :], 0.0) + jnp.where(hit1, probs[1:2, :], 0.0)
        prob = jnp.sum(prob, axis=1, keepdims=True)
        scale[half] = jnp.where(a == 0, 1.0, prob)
    for load in loads:
        load.wait()
    half_width = width // 4
    lot = 16


    def body(i, carry):
        for r in range(2):
            first, second = (
                rows_in[
                    :, pl.ds(pl.multiple_of((2 * r + h) * half_width + i * TILE, TILE), TILE)
                ]
                for h in range(2)
            )
            at = pl.ds(pl.multiple_of(i * TILE, TILE), TILE)
            for g in range(experts // lot):
                part = slice(g * lot * reach, (g + 1) * lot * reach)
                y0 = jnp.dot(low[part, :], first, preferred_element_type=F32)
                y1 = jnp.dot(high[part, :], second, preferred_element_type=F32)
                y0 = y0 * scale[0, part, 0:1]
                y1 = y1 * scale[1, part, 0:1]
                mid = reach // 2
                for j in range(lot):
                    base = j * reach
                    made = [
                        y0[base : base + mid],
                        y0[base + mid : base + reach] + y1[base : base + mid],
                        y1[base + mid : base + reach],
                    ]
                    out_ref[g * lot + j, r, :, at] = jnp.concatenate(made, axis=0).astype(BF)
        return carry

    lax.fori_loop(0, half_width // TILE, body, 0)


def dispatch(routes, probs, tokens, cotangent, experts, cap):
    tok, width = tokens.shape
    half = width // 4
    per = 4 * cap
    rows = experts * per * 2 // 3
    anywhere = pl.BlockSpec(memory_space=pl.ANY)
    return pl.pallas_call(
        functools.partial(dispatch_kernel, cap, experts),
        in_specs=[anywhere] * 4,
        out_specs=held(),
        out_shape=jax.ShapeDtypeStruct((experts, 2, per, half), BF),
        scratch_shapes=[
            pltpu.VMEM((2 * tok, width), BF),
            pltpu.VMEM((rows, 2 * tok), BF),
            pltpu.VMEM((rows, 2 * tok), BF),
            pltpu.VMEM((2, rows, 128), F32),
            pltpu.VMEM((2, tok), jnp.int32),
            pltpu.VMEM((2, tok), F32),
            pltpu.SemaphoreType.DMA((4,)),
        ],
        compiler_params=pltpu.CompilerParams(vmem_limit_bytes=DISPATCH_VMEM),
        cost_estimate=pl.CostEstimate(
            flops=3 * 10**9, bytes_accessed=13 * MIB, transcendentals=0
        ),
        name="dispatch",
    )(routes, probs, tokens, cotangent)


def order_matrix(group, cap, inverse, paired=False):
    n = group * cap * 4
    i = lax.broadcasted_iota(jnp.int32, (n, n), 1 if inverse else 0)
    j = lax.broadcasted_iota(jnp.int32, (n, n), 0 if inverse else 1)
    hk = i // (group * cap)
    rest = i - hk * (group * cap)
    src = rest // cap
    slot = rest - src * cap
    if paired:
        part = src // (group // 2)
        src = 2 * (src - part * (group // 2)) + part
    return jnp.where(src * (4 * cap) + hk * cap + slot == j, 1.0, 0.0).astype(BF)


def unmix(fore, recv_ref, first, columns, group, cap):
    n = group * cap
    span = 4 * n
    made = [[] for _ in range(4)]
    for g in range(first.stop // span - first.start // span):
        rows = slice(first.start + g * span, first.start + (g + 1) * span)
        got = jnp.dot(
            fore, recv_ref[rows, columns], preferred_element_type=F32
        ).astype(BF)
        for k in range(4):
            made[k].append(got[k * n : (k + 1) * n])
    return made


def front_kernel(cap, group, part, rank_ref, recv_ref, w_ref, sum_ref, send_ref):
    total = recv_ref.shape[0] // 2
    columns = sum_ref.shape[1]
    front = columns // 3 * 2
    rank = rank_ref[0]
    fore = order_matrix(group, cap, False)
    sum_ref[...] = jnp.zeros_like(sum_ref)

    def body(i, carry):
        at = pl.ds(pl.multiple_of(i * TILE, TILE), TILE)
        made = unmix(fore, recv_ref, slice(part * total, (part + 1) * total), at, group, cap)
        for h in range(2):
            x = jnp.concatenate(made[2 * h], axis=0)
            c = jnp.concatenate(made[2 * h + 1], axis=0)
            w = w_ref[rank, h, at, :]
            sum_ref[:, :front] += jnp.dot(x, w[:, :front], preferred_element_type=F32)
            sum_ref[:, front:] += jnp.dot(c, w[:, front:], preferred_element_type=F32)
        return carry

    lax.fori_loop(0, recv_ref.shape[1] // TILE, body, 0)
    send_ref[...] = sum_ref[...].astype(BF)


def sort_kernel(cap, group, recv_ref, x_ref, c_ref):
    n = group * cap
    fore = order_matrix(group, cap, False)

    def body(i, carry):
        at = pl.ds(pl.multiple_of(i * TILE, TILE), TILE)
        made = unmix(fore, recv_ref, slice(0, recv_ref.shape[0]), at, group, cap)
        for g in range(len(made[0])):
            rows = slice(g * n, (g + 1) * n)
            for h in range(2):
                x_ref[h, rows, at] = made[2 * h][g]
                c_ref[h, rows, at] = made[2 * h + 1][g]
        return carry

    lax.fori_loop(0, recv_ref.shape[1] // TILE, body, 0)


GROUP = 8


def held():
    return pl.BlockSpec(memory_space=pltpu.VMEM)


def scalars():
    return pl.BlockSpec(memory_space=pltpu.SMEM)


def front_call(rank, recv, weight, cap, part):
    total, half = recv.shape
    columns = weight.shape[-1]
    rows = total // 8
    return pl.pallas_call(
        functools.partial(front_kernel, cap, GROUP, part),
        in_specs=[scalars(), held(), held()],
        out_specs=[held(), held()],
        out_shape=[
            jax.ShapeDtypeStruct((rows, columns), F32),
            jax.ShapeDtypeStruct((rows, columns), BF),
        ],
        compiler_params=pltpu.CompilerParams(vmem_limit_bytes=FRONT_VMEM),
        cost_estimate=pl.CostEstimate(
            flops=2 * 10**9, bytes_accessed=7 * MIB, transcendentals=0
        ),
        name="expert_front",
    )(rank, recv, weight)


def sort_call(recv, cap):
    total, half = recv.shape
    rows = total // 4
    return pl.pallas_call(
        functools.partial(sort_kernel, cap, GROUP),
        in_specs=[held()],
        out_specs=[held(), held()],
        out_shape=[jax.ShapeDtypeStruct((2, rows, half), BF)] * 2,
        compiler_params=pltpu.CompilerParams(vmem_limit_bytes=SORT_VMEM),
        cost_estimate=pl.CostEstimate(
            flops=2 * 10**9, bytes_accessed=19 * MIB, transcendentals=0
        ),
        name="sort_rows",
    )(recv)


def rear_kernel(
    cap, group, piece, rank_ref, x_ref, c_ref, own0, own1, other0, other1, w_ref, first_ref,
    second_ref, out_ref, inner, pre
):
    n = group * cap
    per = 4 * cap
    sets = out_ref.shape[0] // group
    tiles, tile = out_ref.shape[1] - 3, out_ref.shape[3]
    hidden = inner.shape[1]
    rank = rank_ref[0]
    back = order_matrix(group, cap, True)
    total = jnp.concatenate(
        [own0[...] + other0[...].astype(F32), own1[...] + other1[...].astype(F32)], axis=0
    )
    gate = total[:, :hidden]
    up = total[:, hidden : 2 * hidden]
    grad = total[:, 2 * hidden :]
    sig = jax.nn.sigmoid(gate)
    active = gate * sig
    inner[...] = (active * up).astype(BF)
    slope = sig * (1.0 + gate * (1.0 - sig))
    pre[:, :hidden] = (grad * up * slope).astype(BF)
    pre[:, hidden:] = (grad * active).astype(BF)
    contract = (((1,), (1,)), ((), ()))
    lead = (((0,), (0,)), ((), ()))

    def body(i, carry):
        cols = pl.ds(pl.multiple_of(i * tile, tile), tile)
        made = []
        for h in range(2):
            for factor, at in (
                (inner, slice(2 * hidden, 3 * hidden)),
                (pre, slice(0, 2 * hidden)),
            ):
                made.append(
                    lax.dot_general(
                        factor[...], w_ref[rank, h, cols, at], contract,
                        preferred_element_type=F32,
                    ).astype(BF)
                )
        for g in range(sets):
            stack = jnp.concatenate([m[g * n : (g + 1) * n] for m in made], axis=0)
            mixed = jnp.dot(back, stack, preferred_element_type=F32)
            for j in range(group):
                out_ref[g * group + j, i] = mixed[j * per : (j + 1) * per].astype(BF)
        for h in range(2):
            for source, factor, at in (
                (x_ref, pre, slice(0, 2 * hidden)),
                (c_ref, inner, slice(2 * hidden, 3 * hidden)),
            ):
                grad = lax.dot_general(
                    source[h, :, cols], factor[...], lead, preferred_element_type=F32
                )
                m = 0.9 * first_ref[h, cols, at].astype(F32) + 0.1 * grad
                v = 0.95 * second_ref[h, cols, at].astype(F32) + 0.05 * grad * grad
                scale = pl.reciprocal(v * lax.rsqrt(v) + 1e-08)
                step = m * scale + 0.1 * w_ref[rank, h, cols, at].astype(F32)
                count = tile // piece
                for k, value in enumerate((m, v, step)):
                    for j in range(count):
                        out_ref[(h * tiles + i) * count + j, tiles + k, :, at] = value[
                            j * piece : (j + 1) * piece
                        ].astype(BF)
        return carry

    lax.fori_loop(0, tiles, body, 0)


def rear_call(rank, x, c, own, other, weight, first, second, cap, piece):
    rows, half = x.shape[1:]
    columns = weight.shape[-1]
    hidden = columns // 3
    tile = 3 * hidden
    tiles = half // tile
    return pl.pallas_call(
        functools.partial(rear_kernel, cap, GROUP, piece),
        in_specs=[scalars()] + [held()] * 9,
        out_specs=held(),
        scratch_shapes=[pltpu.VMEM((rows, hidden), BF), pltpu.VMEM((rows, 2 * hidden), BF)],
        out_shape=jax.ShapeDtypeStruct((rows // cap, tiles + 3, piece, tile), BF),
        compiler_params=pltpu.CompilerParams(vmem_limit_bytes=REAR_VMEM),
        cost_estimate=pl.CostEstimate(
            flops=7 * 10**9, bytes_accessed=36 * MIB, transcendentals=rows * hidden
        ),
        name="expert_rear",
    )(
        rank, x, c, *own, *other, weight,
        first.reshape(2, half, columns), second.reshape(2, half, columns),
    )


def column(row):
    n = row.shape[1]
    same = lax.broadcasted_iota(jnp.int32, (n, n), 0) == lax.broadcasted_iota(
        jnp.int32, (n, n), 1
    )
    return jnp.sum(jnp.where(same, row, jnp.zeros_like(row)), axis=1, keepdims=True)


def combine_kernel(
    cap, group, experts, route_ref, prob_ref, back_ref, mixed_ref, grad_ref, stage, pick, both,
    mixed, grads, sem
):
    sources, _, per, tile = back_ref.shape
    tok, width = mixed.shape
    half = width // 4
    tiles = half // tile
    m = group // 2 * cap
    rows = experts * cap
    fore = order_matrix(group, cap, False, True)
    slot0, slot1 = slots_of(route_ref[...], experts, cap)
    prob0, prob1 = column(prob_ref[0:1, :]), column(prob_ref[1:2, :])
    ident = lax.broadcasted_iota(jnp.int32, (tok, rows), 1)
    hit0 = ident == column(slot0)
    hit1 = ident == column(slot1)
    pick[:tok, :] = jnp.where(hit0, 1.0, 0.0).astype(BF)
    pick[tok:, :] = jnp.where(hit1, 1.0, 0.0).astype(BF)
    both[...] = jnp.where(hit0 | hit1, 1.0, 0.0).astype(BF)
    sends = []
    for i in range(tiles):
        for g in range(sources // group):
            block = back_ref[g * group : (g + 1) * group, i].reshape(group * per, tile)
            got = jnp.dot(fore, block, preferred_element_type=F32)
            for k in range(4):
                for r in range(2):
                    at = (2 * k + r) * m
                    stage[k, r, g * m : (g + 1) * m, :] = got[at : at + m].astype(BF)
        for r in range(2):
            for h in range(2):
                to = slice((2 * r + h) * half + i * tile, (2 * r + h) * half + (i + 1) * tile)
                out = jnp.dot(pick[...], stage[2 * h, r], preferred_element_type=F32)
                grad = jnp.dot(both[...], stage[2 * h + 1, r], preferred_element_type=F32)
                mixed[:, to] = (out[:tok] * prob0 + out[tok:] * prob1).astype(BF)
                grads[:, to] = grad.astype(BF)
                for k, (source, target) in enumerate(((mixed, mixed_ref), (grads, grad_ref))):
                    at = pl.ds(to.start, tile)
                    send = pltpu.make_async_copy(
                        source.at[:, at], target.at[:, at], sem.at[k, len(sends) // 2]
                    )
                    send.start()
                    sends.append(send)
    for send in sends:
        send.wait()


def combine(routes, probs, back, experts, cap):
    sources, slabs, _, tile = back.shape
    rows = experts * cap
    tok = routes.shape[1]
    width = 4 * (slabs - 3) * tile
    shape = jax.ShapeDtypeStruct((tok, width), BF)
    return pl.pallas_call(
        functools.partial(combine_kernel, cap, GROUP, experts),
        in_specs=[held()] * 3,
        out_specs=[pl.BlockSpec(memory_space=pl.ANY)] * 2,
        out_shape=[shape, shape],
        scratch_shapes=[
            pltpu.VMEM((4, 2, rows, tile), BF),
            pltpu.VMEM((2 * tok, rows), BF),
            pltpu.VMEM((tok, rows), BF),
            pltpu.VMEM((tok, width), BF),
            pltpu.VMEM((tok, width), BF),
            pltpu.SemaphoreType.DMA((2, width // tile)),
        ],
        compiler_params=pltpu.CompilerParams(vmem_limit_bytes=COMBINE_VMEM),
        cost_estimate=pl.CostEstimate(
            flops=6 * 10**9, bytes_accessed=13 * MIB, transcendentals=0
        ),
        name="combine",
    )(routes, probs, back)


def reorder_kernel(place_ref, source, out):
    def body(e, carry):
        for r in range(2):
            out[2 * place_ref[e] + r] = source[2 * e + r, -3:]
        return carry

    lax.fori_loop(0, out.shape[0] // 2, body, 0)


def reorder(array, placement):
    sources, _, piece, columns = array.shape
    return pl.pallas_call(
        reorder_kernel,
        in_specs=[scalars(), held()],
        out_specs=held(),
        out_shape=jax.ShapeDtypeStruct((sources, 3, piece, columns), BF),
        compiler_params=pltpu.CompilerParams(vmem_limit_bytes=4 * MIB),
        cost_estimate=pl.CostEstimate(
            flops=0, bytes_accessed=12 * sources * piece * columns, transcendentals=0
        ),
        name="reorder",
    )(placement, array)


def swap(array, axes):
    return lax.all_to_all(array, axes, split_axis=0, concat_axis=0, tiled=True)


def split_kernel(source, *refs):
    outs, sem = refs[:3], refs[3]
    copies = [
        pltpu.make_async_copy(source.at[:, k], out, sem.at[k])
        for k, out in enumerate(outs)
    ]
    for copy in copies:
        copy.start()
    for copy in copies:
        copy.wait()


def split(moved):
    count, _, piece, columns = moved.shape
    return pl.pallas_call(
        split_kernel,
        in_specs=[held()],
        out_specs=[pl.BlockSpec(memory_space=pl.ANY)] * 3,
        out_shape=[jax.ShapeDtypeStruct((count, piece, columns), BF)] * 3,
        scratch_shapes=[pltpu.SemaphoreType.DMA((3,))],
        compiler_params=pltpu.CompilerParams(vmem_limit_bytes=4 * MIB),
        cost_estimate=pl.CostEstimate(flops=0, bytes_accessed=4 * moved.size, transcendentals=0),
        name="split",
    )(moved)


def local(tokens, cotangent, gate_probs, routes, placement, weights, first_moment, second_moment):
    experts = lax.axis_size("expert")
    tok, width = tokens.shape
    top = routes.shape[1]
    cap = max(2, (3 * tok * top + 2 * experts - 1) // (2 * experts))
    rank = lax.axis_index("dp")
    weight = weights[0]
    rows = weight.shape[0] // 2
    piece = rows // (2 * experts)
    columns = weight.shape[1]
    both = ("expert", "dp")
    together = lax.optimization_barrier

    place = rank.reshape(1).astype(jnp.int32)
    send = dispatch(routes.T, gate_probs.T, tokens, cotangent, experts, cap)
    send, place = together((send, place))
    recv = swap(send.reshape(-1, width // 4), both)
    weight = weight.reshape(2, 2, rows // 2, columns)
    recv, place = together((recv, place))
    own0, out0 = front_call(place, recv, weight, cap, 0)
    recv, own0 = together((recv, own0))
    x, c = sort_call(recv, cap)
    recv, x = together((recv, x))
    own1, out1 = front_call(place, recv, weight, cap, 1)
    other = [lax.ppermute(out, "dp", [(0, 1), (1, 0)]) for out in (out0, out1)]
    sent = rear_call(
        place, x, c, [own0, own1], other, weight, first_moment[0], second_moment[0], cap, piece
    )
    back = swap(sent.reshape(-1, columns), both).reshape(sent.shape)
    ready = reorder(back, placement)
    mixed, token_grad = combine(routes.T, gate_probs.T, back, experts, cap)
    ready, mixed, token_grad = together((ready, mixed, token_grad))
    moved = swap(ready.reshape(-1, columns), both).reshape(ready.shape)
    m, v, step = (array.reshape(1, rows, columns) for array in split(moved))
    return (mixed, token_grad, m, v, step)


def solution(mesh):
    in_specs = (
        P(("expert", "dp"), None),
        P(("expert", "dp"), None),
        P(("expert", "dp"), None),
        P(("expert", "dp"), None),
        P(),
        P("expert", None, None),
        P("expert", "dp", None),
        P("expert", "dp", None),
    )
    out_specs = (
        P(("expert", "dp"), None),
        P(("expert", "dp"), None),
        P("expert", "dp", None),
        P("expert", "dp", None),
        P("expert", "dp", None),
    )
    return jax.shard_map(local, mesh=mesh, in_specs=in_specs, out_specs=out_specs, check_vma=False)
```
